32 devices in a mesh: dp: 8 (over y, x, core), seq: 4 (over z).
Axes of the slice: x: 2, y: 2, z: 4, core: 2. Of those that a mesh axis runs over, the one named last changes fastest.
Arguments:
- tokens_in: bfloat16 [8, 2048, 1024], P('dp', 'seq'), may hold values from -6 to 6
- user_ids: int32 [8, 2048], P('dp'), may hold values from 0 to 3, never falling along the last dimension, each value on 1 to 1024 neighbouring positions
- w_in: bfloat16 [1024, 2048], replicated, may hold values from -0.1875 to 0.1875
- w_out: bfloat16 [512, 1024], replicated, may hold values from -0.25 to 0.25
- cotangent: bfloat16 [8, 2048, 1024], P('dp', 'seq'), may hold values from -6 to 6
Outputs:
- output: bfloat16 [8, 2048, 1024], P('dp', 'seq')
- grad_tokens: bfloat16 [8, 2048, 1024], P('dp', 'seq')
- grad_w_in: float32 [1024, 2048], P(('dp', 'seq'))
- grad_w_out: float32 [512, 1024], P(None, ('dp', 'seq'))
The draws below stay inside these ranges and needn't reach their ends.
Inputs may be any that keep to these rules, and one draw needn't show every extreme that they name: `user_ids`: in each stream the user number never falls; each user holds 1 to 1024 consecutive events and some user holds exactly 1024.
All inputs are finite; a program needn't handle non-finite values.
Results may differ from the reference program's by a relative error of at most 0.015.
Values may be sent and summed in bfloat16 or wider, within the bound.
No kernel may reach another device: no remote copies, remote signals or barrier semaphores. Data moves between devices by JAX's collectives and lax.ppermute only.
A program may use at most 128 MiB of HBM per device.

```python
import math
import jax
import jax.numpy as jnp
import numpy as np
from jax import lax

D = 1024
HEADS = 4
HD = 128
ROWS = 512
USERS = 4
HQ = 512
STREAM = 2048
MOST = 1024
N_DP = 8


def raised(entries, rng, source, target, blocks, factor):
    def block_of(axis_at):
        return (jnp.arange(entries.shape[axis_at]) // (entries.shape[axis_at] // blocks)).reshape((-1,) + (1,) * (entries.ndim - 1 - axis_at))

    first = jax.random.permutation(rng, blocks)[block_of(target)]
    other_side = (block_of(target) + blocks // 2) % blocks
    return jnp.where((block_of(source) == first) | (block_of(source) == other_side), factor * entries, entries)


def steps_of(rng, shape, shards, low, high):
    loudness = 1.0
    for position, blocks in shards:
        draws = jax.random.uniform(jax.random.fold_in(jax.random.fold_in(rng, 6), position), (blocks,), jnp.float32, low / len(shards), high / len(shards))
        loudness = loudness * jnp.repeat(jnp.exp(draws), shape[position] // blocks).reshape((-1,) + (1,) * (len(shape) - 1 - position))
    return loudness


def length_profile(count, total, bound, lean):
    loads = [(1 << 20) // math.isqrt(rank ** lean) + 1 for rank in range(2, count + 1)]
    spare, holding = total - bound - (count - 1), [1] * (count - 1)
    while spare > 0:
        candidates = [i for i in range(count - 1) if holding[i] < bound]
        pool, left = sum([loads[i] for i in candidates]), spare
        for i in candidates:
            extra = min(bound - holding[i], max(1, left * loads[i] // pool), spare)
            holding[i] = holding[i] + extra
            spare = spare - extra
    return np.array([bound] + holding)


def uneven_parts(own_key, amount, total, bound, lean):
    if amount == 2:
        one = jax.random.randint(own_key, (), max(1, total - bound), min(bound, total - 1) + 1)
        return jnp.stack([one, total - one])
    lengths = jnp.asarray(length_profile(amount, total, bound, lean), jnp.int32)
    couples = (amount - 1) // 2
    donor, receiver = lengths[1:1 + 2 * couples:2], lengths[2:2 + 2 * couples:2]
    margin = jnp.minimum(donor - 1, bound - receiver)
    shifted = jax.random.randint(jax.random.fold_in(own_key, 1), (couples,), 0, 1 << 20) % (margin + 1)
    lengths = lengths.at[1:1 + 2 * couples:2].set(donor - shifted).at[2:2 + 2 * couples:2].set(receiver + shifted)
    return lengths[jax.random.permutation(jax.random.fold_in(own_key, 2), amount)]


def gaussian(stream_key, dims, deviation, limit, cuts=(), held_as=jnp.bfloat16):
    result = deviation * jax.random.normal(stream_key, dims, jnp.float32)
    if cuts:
        result = result * steps_of(stream_key, dims, cuts, -0.22, 0.18)
    return jnp.clip(result, -limit, limit).astype(held_as)


def noise_with(stream_key, dims, scale, bound, shards, heavy, kind=jnp.bfloat16):
    array = scale * jax.random.normal(stream_key, dims, jnp.float32)
    if shards:
        array = array * steps_of(stream_key, dims, shards, -0.22, 0.18)
    return jnp.clip(raised(array, jax.random.fold_in(stream_key, 3), *heavy), -bound, bound).astype(kind)


def setup_inputs(seed: int = 0) -> dict:
    keys = jax.random.split(jax.random.key(seed), 6)
    tokens_in = noise_with(keys[0], (N_DP, STREAM, D), 1.0, 6.0, ((0, 8), (1, 4)), (1, 2, 4, 2.0))
    user_ids = jax.vmap(lambda own: jnp.searchsorted(jnp.cumsum(uneven_parts(own, USERS, STREAM, MOST, 2)), jnp.arange(STREAM), side="right"))(jax.random.split(keys[1], N_DP)).reshape((N_DP, STREAM)).astype(jnp.int32)
    w_in = gaussian(keys[2], (D, 4 * HQ), D ** -0.5, 0.1875)
    w_out = gaussian(keys[3], (HQ, D), HQ ** -0.5, 0.25)
    cotangent = noise_with(keys[4], (N_DP, STREAM, D), 1.0, 6.0, ((0, 8), (1, 4)), (1, 2, 4, 2.0))
    return dict(tokens_in=tokens_in, user_ids=user_ids, w_in=w_in, w_out=w_out, cotangent=cotangent)


epsilon = 1e-05

def normalize(values):
    center = values - lax.optimization_barrier(jnp.mean(values, axis=-1, keepdims=True))
    inverse = lax.rsqrt(lax.optimization_barrier(jnp.mean(center * center, axis=-1, keepdims=True)) + epsilon)
    return center * inverse

def norm_back(values, upstream):
    center = values - lax.optimization_barrier(jnp.mean(values, axis=-1, keepdims=True))
    inverse = lax.rsqrt(lax.optimization_barrier(jnp.mean(center * center, axis=-1, keepdims=True)) + epsilon)
    scaled = center * inverse
    return inverse * (upstream - lax.optimization_barrier(jnp.mean(upstream, axis=-1, keepdims=True)) - scaled * lax.optimization_barrier(jnp.mean(upstream * scaled, axis=-1, keepdims=True)))

def silu_slope(values):
    sigma = jax.nn.sigmoid(values)
    return sigma * (1.0 + values * (1.0 - sigma))

def reference(tokens_in, user_ids, w_in, w_out, cotangent):
    scale = 1.0 / math.sqrt(HD)
    window = MOST + ROWS
    blocks = STREAM // ROWS

    def one_stream(carry, inputs):
        tokens, id_table, upstream = inputs
        tokens_f = tokens.astype(jnp.float32)
        normed = normalize(tokens_f).astype(jnp.bfloat16)
        hidden = jnp.dot(normed, w_in, preferred_element_type=jnp.float32)
        active = jax.nn.silu(hidden).astype(jnp.bfloat16)
        gate_u = active[:, :HQ]
        value_heads = active[:, HQ:2 * HQ].astype(jnp.float32).reshape(STREAM, HEADS, HD)
        query_heads = active[:, 2 * HQ:3 * HQ].astype(jnp.float32).reshape(STREAM, HEADS, HD)
        key_heads = active[:, 3 * HQ:].astype(jnp.float32).reshape(STREAM, HEADS, HD)

        def block_parts(index):
            q_start = (index * ROWS).astype(jnp.int32)
            k_start = jnp.clip(q_start - MOST, 0, STREAM - window).astype(jnp.int32)
            query_block = lax.dynamic_slice_in_dim(query_heads, q_start, ROWS, 0)
            key_block = lax.dynamic_slice_in_dim(key_heads, k_start, window, 0)
            value_block = lax.dynamic_slice_in_dim(value_heads, k_start, window, 0)
            q_users = lax.dynamic_slice_in_dim(id_table, q_start, ROWS, 0)
            k_users = lax.dynamic_slice_in_dim(id_table, k_start, window, 0)
            q_pos = q_start + jnp.arange(ROWS, dtype=jnp.int32)
            k_pos = k_start + jnp.arange(window, dtype=jnp.int32)
            allowed = (q_users[:, None] == k_users[None, :]) & (k_pos[None, :] <= q_pos[:, None])
            mask = allowed.astype(jnp.float32)[None]
            scores = jnp.einsum('qhd,khd->hqk', query_block, key_block) * scale
            weights = (jax.nn.silu(scores) * mask).astype(jnp.bfloat16)
            return (q_start, k_start, query_block, key_block, value_block, mask, scores, weights)

        def forward_block(index):
            parts = block_parts(index)
            return jnp.einsum('hqk,khd->qhd', parts[7].astype(jnp.float32), parts[4])
        attended = lax.map(forward_block, jnp.arange(blocks, dtype=jnp.int32)).reshape(STREAM, HQ)
        normed_out = normalize(attended)
        gated = (normed_out * gate_u.astype(jnp.float32)).astype(jnp.bfloat16)
        output = (jnp.dot(gated, w_out, preferred_element_type=jnp.float32) + tokens_f).astype(jnp.bfloat16)
        grad_w_out = jnp.dot(gated.T, upstream, preferred_element_type=jnp.float32)
        grad_gated = jnp.dot(upstream, w_out.T, preferred_element_type=jnp.float32)
        grad_u = grad_gated * normed_out
        grad_normed = grad_gated * gate_u.astype(jnp.float32)
        grad_attended = norm_back(attended, grad_normed).astype(jnp.bfloat16)
        grad_heads = grad_attended.astype(jnp.float32).reshape(STREAM, HEADS, HD)

        def backward_block(state, index):
            grad_k, grad_v = state
            q_start, k_start, query_block, key_block, value_block, mask, scores, weights = block_parts(index)
            grad_block = lax.dynamic_slice_in_dim(grad_heads, q_start, ROWS, 0)
            part_v = jnp.einsum('hqk,qhd->khd', weights.astype(jnp.float32), grad_block)
            grad_weights = jnp.einsum('qhd,khd->hqk', grad_block, value_block)
            grad_scores = (grad_weights * silu_slope(scores) * mask).astype(jnp.bfloat16).astype(jnp.float32)
            part_q = jnp.einsum('hqk,khd->qhd', grad_scores, key_block) * scale
            part_k = jnp.einsum('hqk,qhd->khd', grad_scores, query_block) * scale
            grad_k = lax.dynamic_update_slice_in_dim(grad_k, lax.dynamic_slice_in_dim(grad_k, k_start, window, 0) + part_k, k_start, 0)
            grad_v = lax.dynamic_update_slice_in_dim(grad_v, lax.dynamic_slice_in_dim(grad_v, k_start, window, 0) + part_v, k_start, 0)
            return ((grad_k, grad_v), part_q)
        zero_heads = jnp.zeros((STREAM, HEADS, HD), jnp.float32)
        (grad_k, grad_v), grad_q = lax.scan(backward_block, (zero_heads, zero_heads), jnp.arange(blocks, dtype=jnp.int32))
        grad_q = grad_q.reshape(STREAM, HQ)
        grad_all = jnp.concatenate([grad_u, grad_v.reshape(STREAM, HQ), grad_q, grad_k.reshape(STREAM, HQ)], axis=1)
        grad_hidden = (grad_all * silu_slope(hidden)).astype(jnp.bfloat16)
        grad_w_in = jnp.dot(normed.T, grad_hidden, preferred_element_type=jnp.float32)
        grad_normed_in = jnp.dot(grad_hidden, w_in.T, preferred_element_type=jnp.float32)
        grad_tokens = (norm_back(tokens_f, grad_normed_in) + upstream.astype(jnp.float32)).astype(jnp.bfloat16)
        total_in, total_out = carry
        return ((total_in + grad_w_in, total_out + grad_w_out), (output, grad_tokens))
    start = (jnp.zeros((D, 4 * HQ), jnp.float32), jnp.zeros((HQ, D), jnp.float32))
    (total_in, total_out), (output, grad_tokens) = lax.scan(one_stream, start, (tokens_in, user_ids, cotangent))
    return (output, grad_tokens, total_in, total_out)
```

```python
import functools
import math

import jax
import jax.numpy as jnp
from jax import lax
from jax.experimental import pallas as pl
from jax.experimental.pallas import tpu as pltpu
from jax.sharding import PartitionSpec as P

HEADS = 4
HD = 128
HALF_SCALE = 0.5 / math.sqrt(HD)
SCALE = 1.0 / math.sqrt(HD)
EPSILON = 1e-05
BF16 = jnp.bfloat16
F32 = jnp.float32
VMEM = pl.BlockSpec(memory_space=pltpu.VMEM)
SMEM = pl.BlockSpec(memory_space=pltpu.SMEM)


def shift(value, by):
    devices = lax.axis_size("seq")
    pairs = [(i, i + by) for i in range(devices) if 0 <= i + by < devices]
    return lax.ppermute(value, "seq", pairs)


def swap(value, axis, bit):
    return lax.ppermute(value, axis, [(i, i ^ bit) for i in range(lax.axis_size(axis))])


def call(kernel, outs, args, specs=None, scratch=(), flops=0, nbytes=0, name=None):
    return pl.pallas_call(
        kernel,
        grid=(1,),
        out_shape=outs,
        in_specs=specs or [VMEM] * len(args),
        out_specs=jax.tree.map(lambda _: VMEM, outs),
        scratch_shapes=scratch,
        compiler_params=pltpu.CompilerParams(vmem_limit_bytes=40 << 20),
        cost_estimate=pl.CostEstimate(flops=flops, bytes_accessed=nbytes, transcendentals=0),
        name=name,
    )(*args)


def columns(rows, width, block):
    return pl.BlockSpec((rows, width), lambda i: (0, block))


def like(rows, width, kind):
    return jax.ShapeDtypeStruct((rows, width), kind)


def dot(a, b):
    return jnp.dot(a, b, preferred_element_type=F32)


def dot_nt(a, b):
    return lax.dot_general(a, b, (((1,), (1,)), ((), ())), preferred_element_type=F32)


def dot_tn(a, b):
    return lax.dot_general(a, b, (((0,), (0,)), ((), ())), preferred_element_type=F32)


def centred(values):
    center = values - jnp.mean(values, axis=-1, keepdims=True)
    inverse = lax.rsqrt(jnp.mean(center * center, axis=-1, keepdims=True) + EPSILON)
    return center * inverse, inverse


def back(scaled, inverse, upstream):
    return inverse * (
        upstream
        - jnp.mean(upstream, axis=-1, keepdims=True)
        - scaled * jnp.mean(upstream * scaled, axis=-1, keepdims=True)
    )


def silu_and_slope(half):
    bend = 1.0 + jnp.tanh(half)
    value = half * bend
    return value, 0.5 * (bend + value * (2.0 - bend))


def project_kernel(raw, blocks, x_ref, *refs):
    w_refs, refs = refs[:blocks], refs[blocks:]
    if raw:
        normed_ref, refs = refs[0], refs[1:]
        normed_ref[...] = centred(x_ref[...].astype(F32))[0].astype(BF16)
    else:
        normed_ref = x_ref
    slope_ref, act_refs = refs[0], refs[1:]
    width = slope_ref.shape[1] // blocks
    for b in range(blocks):
        value, slope = silu_and_slope(0.5 * dot(normed_ref[...], w_refs[b][...]))
        act_refs[b][...] = value.astype(BF16)
        slope_ref[:, b * width : (b + 1) * width] = slope.astype(BF16)


def project(x, w_in, blocks, raw):
    n, d = x.shape
    width = w_in.shape[1] // 4
    outs = [like(n, d, BF16)] if raw else []
    outs += [like(n, width * len(blocks), BF16)] + [like(n, width, BF16)] * len(blocks)
    return call(
        functools.partial(project_kernel, raw, len(blocks)),
        outs,
        [x] + [w_in] * len(blocks),
        [VMEM] + [columns(d, width, b) for b in blocks],
        flops=2 * n * d * width * len(blocks),
        nbytes=2 * n * d + 2 * d * width * len(blocks),
        name="project",
    )


def forward_kernel(causal, more, q_ref, k_ref, v_ref, uq_ref, uk_ref, *refs):
    add_ref, out_ref = (refs[0], refs[1]) if more else (None, refs[0])
    n = q_ref.shape[0]
    step = n // 2
    for start in range(0, n, step):
        rows = slice(start, start + step)
        keys = slice(0, start + step if causal else n)
        width = keys.stop
        mask = uq_ref[rows, :] == uk_ref[:, keys]
        if causal:
            mask &= lax.broadcasted_iota(jnp.int32, (step, width), 1) <= start + lax.broadcasted_iota(
                jnp.int32, (step, width), 0
            )
        for h in range(HEADS):
            cols = slice(h * HD, (h + 1) * HD)
            half = dot_nt(q_ref[rows, cols], k_ref[keys, cols]) * HALF_SCALE
            weights = jnp.where(mask, half * (1.0 + jnp.tanh(half)), 0.0).astype(BF16)
            part = dot(weights, v_ref[keys, cols])
            if more:
                part = part + add_ref[rows, cols]
            out_ref[rows, cols] = part.astype(out_ref.dtype)


def forward(q, k, v, uq, uk, add=None, causal=False, kind=F32):
    n, width = q.shape
    return call(
        functools.partial(forward_kernel, causal, add is not None),
        like(n, width, kind),
        [q, k, v, uq, uk] + ([] if add is None else [add]),
        flops=4 * n * n * width,
        nbytes=10 * n * width,
        name="forward",
    )


def backward_kernel(causal, more_q, more_k, final, q_ref, k_ref, v_ref, g_ref, uq_ref, uk_ref, *refs):
    refs = list(refs)
    add_q_ref = refs.pop(0) if more_q else None
    add_k_ref = refs.pop(0) if more_k else None
    slope_ref = refs.pop(0) if final else None
    gq_ref, gk_ref = refs.pop(0), refs.pop(0)
    sum_ref = refs.pop(0) if final else gk_ref
    n, width = q_ref.shape
    step = n // 2
    for c, start in enumerate(range(n - step, -1, -step)):
        rows = slice(start, start + step)
        keys = slice(0, start + step if causal else n)
        mask = uk_ref[keys, :] == uq_ref[:, rows]
        if causal:
            mask &= lax.broadcasted_iota(
                jnp.int32, (keys.stop, step), 0
            ) <= start + lax.broadcasted_iota(jnp.int32, (keys.stop, step), 1)
        for h in range(HEADS):
            cols = slice(h * HD, (h + 1) * HD)
            k_cols = slice(width + h * HD, width + (h + 1) * HD)
            half = dot_nt(k_ref[keys, cols], q_ref[rows, cols]) * HALF_SCALE
            value, slope = silu_and_slope(half)
            weights = jnp.where(mask, value, 0.0).astype(BF16)
            grads = dot_nt(v_ref[keys, cols], g_ref[rows, cols]) * slope
            grads = jnp.where(mask, grads, 0.0).astype(BF16)
            part_v = dot(weights, g_ref[rows, cols])
            part_k = dot(grads, q_ref[rows, cols]) * SCALE
            part_q = dot_tn(grads, k_ref[keys, cols]) * SCALE
            if more_q:
                part_q = part_q + add_q_ref[rows, cols]
            gq_ref[rows, cols] = part_q.astype(gq_ref.dtype)
            if c > 0:
                part_v = part_v + sum_ref[keys, cols]
                part_k = part_k + sum_ref[keys, k_cols]
            elif more_k:
                part_v = part_v + add_k_ref[keys, cols]
                part_k = part_k + add_k_ref[keys, k_cols]
            sum_ref[keys, cols] = part_v
            sum_ref[keys, k_cols] = part_k
    if final:
        gk_ref[...] = (sum_ref[...] * slope_ref[...].astype(F32)).astype(BF16)


def backward(q, k, v, grads, uq, uk, add_q=None, add_k=None, slope=None, causal=False, kind=F32):
    n, width = q.shape
    final = slope is not None
    optional = [x for x in (add_q, add_k, slope) if x is not None]
    return call(
        functools.partial(backward_kernel, causal, add_q is not None, add_k is not None, final),
        [like(n, width, kind), like(n, 2 * width, BF16 if final else F32)],
        [q, k, v, grads, uq, uk] + optional,
        scratch=[pltpu.VMEM((n, 2 * width), F32)] if final else [],
        flops=10 * n * n * width,
        nbytes=20 * n * width,
        name="backward",
    )


def gate_kernel(*refs):
    refs, (ga_ref, gated_ref, gu_ref) = refs[:-3], refs[-3:]
    own_ref, far_refs, (gg_ref, u_ref, slope_ref) = refs[0], refs[1:-3], refs[-3:]
    attended = own_ref[...]
    for far_ref in far_refs:
        attended = attended + far_ref[...].astype(F32)
    normed, inverse = centred(attended)
    gate = u_ref[...].astype(F32)
    grad = gg_ref[...]
    ga_ref[...] = back(normed, inverse, grad * gate).astype(BF16)
    gated_ref[...] = (normed * gate).astype(BF16)
    width = u_ref.shape[1]
    gu_ref[...] = (grad * normed * slope_ref[:, :width].astype(F32)).astype(BF16)


def product_kernel(x_ref, w_ref, out_ref):
    out_ref[...] = dot_nt(x_ref[...], w_ref[...]).astype(out_ref.dtype)


def output_kernel(gated_ref, w_ref, tokens_ref, out_ref):
    out_ref[...] = (dot(gated_ref[...], w_ref[...]) + tokens_ref[...].astype(F32)).astype(BF16)


def far_kernel(x_ref, wv_ref, wk_ref, out_ref):
    width = wv_ref.shape[1]
    out_ref[...] = (
        dot_nt(x_ref[:, :width], wv_ref[...]) + dot_nt(x_ref[:, width:], wk_ref[...])
    ).astype(out_ref.dtype)


def near_kernel(gu_ref, gvk_ref, gq_ref, wu_ref, wv_ref, wq_ref, wk_ref, out_ref):
    width = wv_ref.shape[1]
    out_ref[...] = (
        dot_nt(gu_ref[...], wu_ref[...])
        + dot_nt(gvk_ref[:, :width], wv_ref[...])
        + dot_nt(gq_ref[...], wq_ref[...])
        + dot_nt(gvk_ref[:, width:], wk_ref[...])
    )


def tokens_kernel(tokens_ref, cotangent_ref, near_ref, *refs):
    grad = near_ref[...]
    for far_ref in refs[:-1]:
        grad = grad + far_ref[...].astype(F32)
    scaled, inverse = centred(tokens_ref[...].astype(F32))
    refs[-1][...] = (back(scaled, inverse, grad) + cotangent_ref[...].astype(F32)).astype(BF16)


def query_kernel(gq_ref, slope_ref, *refs):
    grad = gq_ref[...]
    for far_ref in refs[:-1]:
        grad = grad + far_ref[...].astype(F32)
    refs[-1][...] = (grad * slope_ref[...].astype(F32)).astype(BF16)


def orders(dp):
    bits = dp.bit_length() - 1
    return list(range(bits)), [0] + list(range(bits - 1, 0, -1))


def relative(slot, order):
    bits = len(order)
    return sum(((slot >> (bits - 1 - p)) & 1) << order[p] for p in range(bits))


def weight_kernel(dp, half, parts, place_ref, *refs):
    out_ref = refs[-1]
    n_slots, rows = out_ref.shape[1], out_ref.shape[2]
    taken = 0
    for part, (order, pairs) in enumerate(zip(orders(dp), parts)):
        total = None
        for lo, hi in pairs:
            x_ref, g_ref = refs[taken], refs[taken + 1]
            taken += 2
            blocks = []
            for slot in range(half * n_slots, (half + 1) * n_slots):
                block = place_ref[0] ^ relative(slot, order)
                blocks.append(x_ref[:, pl.ds(pl.multiple_of(block * rows, rows), rows)])
            term = dot_tn(jnp.concatenate(blocks, axis=1), g_ref[:, lo:hi])
            total = term if total is None else total + term
        out_ref[part] = total.astype(BF16).reshape(out_ref.shape[1:])


def weight_half(place, parts, half):
    dp = lax.axis_size("dp")
    d = parts[0][0][0].shape[1]
    rows = d // dp
    width = parts[0][0][3] - parts[0][0][2]
    if rows % 128:
        out = []
        for order, pairs in zip(orders(dp), parts):
            total = sum(dot_tn(x, g[:, lo:hi]) for x, g, lo, hi in pairs).astype(BF16)
            slots = range(half * dp // 2, (half + 1) * dp // 2)
            out.append(
                jnp.stack(
                    [
                        lax.dynamic_slice_in_dim(total, (place[0] ^ relative(s, order)) * rows, rows)
                        for s in slots
                    ]
                )
            )
        return jnp.stack(out)
    args = [a for pairs in parts for x, g, _, _ in pairs for a in (x, g)]
    n = args[0].shape[0]
    return call(
        functools.partial(
            weight_kernel, dp, half, [[(lo, hi) for _, _, lo, hi in pairs] for pairs in parts]
        ),
        jax.ShapeDtypeStruct((2, dp // 2, rows, width), BF16),
        [place] + args,
        [SMEM] + [VMEM] * len(args),
        flops=n * d * width * len(args) // 2,
        nbytes=2 * d * width,
        name="weights",
    )


def scatter(place, parts):
    dp, n_seq = lax.axis_size("dp"), lax.axis_size("seq")
    arrived = swap(weight_half(place, parts, 1), "dp", 1)
    kept = weight_half(place, parts, 0)
    held = []
    for part, order in enumerate(orders(dp)):
        mine, other = kept[part], arrived[part]
        for bit in order[1:]:
            half = mine.shape[0] // 2
            send = (mine[half:].astype(F32) + other[half:].astype(F32)).astype(BF16)
            mine = (mine[:half].astype(F32) + other[:half].astype(F32)).astype(BF16)
            other = swap(send, "dp", 1 << bit)
        held.append((mine, other))
    rows, width = kept.shape[2] // n_seq, kept.shape[3]

    def chunk(index):
        return jnp.stack(
            [
                lax.dynamic_slice(a, (0, index * rows, 0), (1, rows, width))[0].astype(F32)
                + lax.dynamic_slice(b, (0, index * rows, 0), (1, rows, width))[0].astype(F32)
                for a, b in held
            ]
        )

    far = [swap(chunk(place[1] ^ r).astype(BF16), "seq", r) for r in range(1, n_seq)]
    total = chunk(place[1])
    for value in far:
        total = total + value.astype(F32)
    return total[0], total[1]


def local(tokens_in, user_ids, w_in, w_out, cotangent):
    tokens, id_table, upstream = tokens_in[0], user_ids[0], cotangent[0]
    n, d = tokens.shape
    width = w_out.shape[0]
    n_seq = lax.axis_size("seq")
    span = n_seq // 2
    up = (span + 1) // 2
    down = span - up
    me = lax.axis_index("seq")
    place = jnp.stack([lax.axis_index("dp"), me]).astype(jnp.int32)

    def users_of(block):
        valid = (block >= 0) & (block < n_seq)
        ids = lax.dynamic_slice_in_dim(id_table, jnp.clip(block, 0, n_seq - 1) * n, n)
        ids = jnp.where(valid, ids, -1)
        return ids.reshape(n, 1), ids.reshape(1, n)

    far_tokens = [shift(tokens, by) for by in range(1, up + 1)]
    normed, slope_q, query = project(tokens, w_in, [2], True)
    far_query = shift(query, -up) if down else None
    slope_uvk, gate, values, keys = project(normed, w_in, [0, 1, 3], False)
    slope_vk = slope_uvk[:, width:]
    grad_gated = call(
        product_kernel, like(n, width, F32), [upstream, w_out], flops=2 * n * d * width, name="gated"
    )
    my_col, my_row = users_of(me)
    up_col, up_row = users_of(me + up)
    attended = forward(query, keys, values, my_col, my_row, causal=True)

    pieces = []
    for by in range(1, up + 1):
        far_normed, far_slope, far_values, far_keys = project(
            far_tokens[by - 1], w_in, [1, 3], True
        )
        pieces.append((far_normed, far_slope, far_values, far_keys, *users_of(me - by)))
    if down:
        partial = None
        for by in range(1, down + 1):
            _, _, far_values, far_keys, _, row = pieces[by - 1]
            partial = forward(
                far_query, far_keys, far_values, up_col, row, partial, kind=BF16 if by == down else F32
            )
        far_attended = [shift(partial, up)]
    else:
        far_attended = []
    for _, _, far_values, far_keys, _, row in pieces:
        attended = forward(query, far_keys, far_values, my_col, row, attended)

    grad_attended, gated, grad_u = call(
        gate_kernel,
        [like(n, width, BF16)] * 3,
        [attended, *far_attended, grad_gated, gate, slope_uvk],
        name="gate",
    )
    far_grad = shift(grad_attended, -up) if down else None
    out_w, grad_in_u = scatter(
        place, [[(upstream, gated, 0, width)], [(normed, grad_u, 0, width)]]
    )
    output = call(
        output_kernel, like(n, d, BF16), [gated, w_out, tokens], flops=2 * n * d * width, name="output"
    )

    grad_q, grad_vk = backward(
        query, keys, values, grad_attended, my_row, my_col, slope=slope_vk, causal=True
    )
    far_sums = []
    for by, (_, slope, far_values, far_keys, col, _) in enumerate(pieces, 1):
        grad_q, far_sum = backward(
            query, far_keys, far_values, grad_attended, my_row, col, add_q=grad_q,
            slope=None if by <= down else slope,
        )
        far_sums.append(far_sum)
    far_q = None
    for by in range(1, down + 1):
        _, slope, far_values, far_keys, col, _ = pieces[by - 1]
        far_q, far_sums[by - 1] = backward(
            far_query, far_keys, far_values, far_grad, up_row, col, add_q=far_q,
            add_k=far_sums[by - 1], slope=slope, kind=BF16 if by == down else F32,
        )
    far_parts = []
    for by, grad in enumerate(far_sums, 1):
        part = call(
            far_kernel,
            like(n, d, BF16),
            [grad, w_in, w_in],
            [VMEM, columns(d, width, 1), columns(d, width, 3)],
            flops=4 * n * d * width,
            name="far",
        )
        far_parts.append(shift(part, -by))
    back_q = [shift(far_q, up)] if down else []
    held = [(normed, grad_vk)] + [(p[0], g) for p, g in zip(pieces, far_sums)]
    grad_in_v, grad_in_k = scatter(
        place,
        [[(x, g, 0, width) for x, g in held], [(x, g, width, 2 * width) for x, g in held]],
    )
    grad_q = call(query_kernel, like(n, width, BF16), [grad_q, slope_q, *back_q], name="query")
    q_left, q_right = scatter(
        place, [[(normed, grad_q, 0, width // 2)], [(normed, grad_q, width // 2, width)]]
    )
    near = call(
        near_kernel,
        like(n, d, F32),
        [grad_u, grad_vk, grad_q] + [w_in] * 4,
        [VMEM] * 3 + [columns(d, width, b) for b in range(4)],
        flops=8 * n * d * width,
        name="near",
    )
    grad_tokens = call(
        tokens_kernel, like(n, d, BF16), [tokens, upstream, near, *far_parts], name="tokens"
    )
    total_in = jnp.concatenate([grad_in_u, grad_in_v, q_left, q_right, grad_in_k], axis=1)
    return (output[None], grad_tokens[None], total_in, out_w.T)


def solution(mesh):
    in_specs = (P("dp", "seq", None), P("dp", None), P(), P(), P("dp", "seq", None))
    out_specs = (
        P("dp", "seq", None),
        P("dp", "seq", None),
        P(("dp", "seq"), None),
        P(None, ("dp", "seq")),
    )
    return jax.shard_map(local, mesh=mesh, in_specs=in_specs, out_specs=out_specs, check_vma=False)
```

```python
import functools
import math

import jax
import jax.numpy as jnp
from jax import lax
from jax.experimental import pallas as pl
from jax.experimental.pallas import tpu as pltpu
from jax.sharding import PartitionSpec as P

HEADS = 4
HD = 128
HALF_SCALE = 0.5 / math.sqrt(HD)
SCALE = 1.0 / math.sqrt(HD)
EPSILON = 1e-05
BF16 = jnp.bfloat16
F32 = jnp.float32
VMEM = pl.BlockSpec(memory_space=pltpu.VMEM)
SMEM = pl.BlockSpec(memory_space=pltpu.SMEM)


def shift(value, by):
    devices = lax.axis_size("seq")
    pairs = [(i, i + by) for i in range(devices) if 0 <= i + by < devices]
    return lax.ppermute(value, "seq", pairs)


def call(kernel, outs, args, specs=None, scratch=(), flops=0, nbytes=0, name=None, after=()):
    first, last = len(args), len(args) + len(after)

    def body(*refs):
        kernel(*refs[:first], *refs[last:])

    return pl.pallas_call(
        body,
        grid=(1,),
        out_shape=outs,
        in_specs=(specs or [VMEM] * first) + [pl.BlockSpec(memory_space=pl.ANY)] * len(after),
        out_specs=jax.tree.map(lambda _: VMEM, outs),
        scratch_shapes=scratch,
        compiler_params=pltpu.CompilerParams(vmem_limit_bytes=40 << 20),
        cost_estimate=pl.CostEstimate(flops=flops, bytes_accessed=nbytes, transcendentals=0),
        name=name,
    )(*args, *after)


def columns(rows, width, block):
    return pl.BlockSpec((rows, width), lambda i: (0, block))


def like(rows, width, kind):
    return jax.ShapeDtypeStruct((rows, width), kind)


def dot(a, b):
    return jnp.dot(a, b, preferred_element_type=F32)


def dot_nt(a, b):
    return lax.dot_general(a, b, (((1,), (1,)), ((), ())), preferred_element_type=F32)


def dot_tn(a, b):
    return lax.dot_general(a, b, (((0,), (0,)), ((), ())), preferred_element_type=F32)


def centred(values):
    center = values - jnp.mean(values, axis=-1, keepdims=True)
    inverse = lax.rsqrt(jnp.mean(center * center, axis=-1, keepdims=True) + EPSILON)
    return center * inverse, inverse


def back(scaled, inverse, upstream):
    return inverse * (
        upstream
        - jnp.mean(upstream, axis=-1, keepdims=True)
        - scaled * jnp.mean(upstream * scaled, axis=-1, keepdims=True)
    )


def silu_and_slope(half):
    bend = 1.0 + jnp.tanh(half)
    value = half * bend
    return value, 0.5 * (bend + value * (2.0 - bend))


def project_kernel(raw, blocks, x_ref, *refs):
    w_refs, refs = refs[:blocks], refs[blocks:]
    if raw:
        normed_ref, refs = refs[0], refs[1:]
        normed_ref[...] = centred(x_ref[...].astype(F32))[0].astype(BF16)
    else:
        normed_ref = x_ref
    slope_ref, act_refs = refs[0], refs[1:]
    width = slope_ref.shape[1] // blocks
    for b in range(blocks):
        value, slope = silu_and_slope(0.5 * dot(normed_ref[...], w_refs[b][...]))
        act_refs[b][...] = value.astype(BF16)
        slope_ref[:, b * width : (b + 1) * width] = slope.astype(BF16)


def project(x, w_in, blocks, raw, after=()):
    n, d = x.shape
    width = w_in.shape[1] // 4
    outs = [like(n, d, BF16)] if raw else []
    outs += [like(n, width * len(blocks), BF16)] + [like(n, width, BF16)] * len(blocks)
    return call(
        functools.partial(project_kernel, raw, len(blocks)),
        outs,
        [x] + [w_in] * len(blocks),
        [VMEM] + [columns(d, width, b) for b in blocks],
        flops=2 * n * d * width * len(blocks),
        nbytes=2 * n * d + 2 * d * width * len(blocks),
        name="project",
        after=after,
    )


def squares(n, causal, flags_ref, body):
    step = n // 2
    for c, rows in enumerate(range(0, n, step)):
        for e, keys in enumerate(range(0, n, step)):
            run = functools.partial(body, slice(rows, rows + step), slice(keys, keys + step))
            if not causal:
                pl.when(flags_ref[2 * c + e] != 0)(functools.partial(run, False))
            elif e <= c:
                run(e == c)


def forward_kernel(causal, more, flags_ref, q_ref, k_ref, v_ref, uq_ref, uk_ref, *refs):
    refs = list(refs)
    add_ref = refs.pop(0) if more else None
    out_ref = refs.pop(0)
    sum_ref = refs.pop(0) if refs else out_ref
    sum_ref[...] = add_ref[...] if more else jnp.zeros_like(sum_ref)

    def square(rows, keys, diagonal):
        mask = uq_ref[rows, :] == uk_ref[:, keys]
        if diagonal:
            mask &= lax.broadcasted_iota(jnp.int32, mask.shape, 1) <= lax.broadcasted_iota(
                jnp.int32, mask.shape, 0
            )
        for h in range(HEADS):
            cols = slice(h * HD, (h + 1) * HD)
            half = dot_nt(q_ref[rows, cols], k_ref[keys, cols]) * HALF_SCALE
            weights = jnp.where(mask, half * (1.0 + jnp.tanh(half)), 0.0).astype(BF16)
            sum_ref[rows, cols] += dot(weights, v_ref[keys, cols])

    squares(q_ref.shape[0], causal, flags_ref, square)
    if sum_ref is not out_ref:
        out_ref[...] = sum_ref[...].astype(out_ref.dtype)


def forward(flags, q, k, v, uq, uk, add=None, causal=False, kind=F32, after=()):
    n, width = q.shape
    optional = [] if add is None else [add]
    return call(
        functools.partial(forward_kernel, causal, add is not None),
        like(n, width, kind),
        [flags, q, k, v, uq, uk] + optional,
        [SMEM] + [VMEM] * (5 + len(optional)),
        scratch=[] if kind == F32 else [pltpu.VMEM((n, width), F32)],
        flops=4 * n * n * width,
        nbytes=10 * n * width,
        name="forward",
        after=after,
    )


def backward_kernel(causal, given, flags_ref, q_ref, k_ref, v_ref, g_ref, uq_ref, uk_ref, *refs):
    refs = list(refs)
    add_q_ref, add_k_ref, slope_q_ref, slope_k_ref = [refs.pop(0) if x else None for x in given]
    gq_ref, gk_ref = refs.pop(0), refs.pop(0)
    sum_q_ref = gq_ref if slope_q_ref is None else refs.pop(0)
    sum_k_ref = gk_ref if slope_k_ref is None else refs.pop(0)
    width = q_ref.shape[1]
    sum_q_ref[...] = jnp.zeros_like(sum_q_ref) if add_q_ref is None else add_q_ref[...]
    sum_k_ref[...] = jnp.zeros_like(sum_k_ref) if add_k_ref is None else add_k_ref[...]

    def square(rows, keys, diagonal):
        mask = uk_ref[keys, :] == uq_ref[:, rows]
        if diagonal:
            mask &= lax.broadcasted_iota(jnp.int32, mask.shape, 0) <= lax.broadcasted_iota(
                jnp.int32, mask.shape, 1
            )
        for h in range(HEADS):
            cols = slice(h * HD, (h + 1) * HD)
            k_cols = slice(width + h * HD, width + (h + 1) * HD)
            half = dot_nt(k_ref[keys, cols], q_ref[rows, cols]) * HALF_SCALE
            value, slope = silu_and_slope(half)
            weights = jnp.where(mask, value, 0.0).astype(BF16)
            grads = dot_nt(v_ref[keys, cols], g_ref[rows, cols]) * slope
            grads = jnp.where(mask, grads, 0.0).astype(BF16)
            sum_k_ref[keys, cols] += dot(weights, g_ref[rows, cols])
            sum_k_ref[keys, k_cols] += dot(grads, q_ref[rows, cols]) * SCALE
            sum_q_ref[rows, cols] += dot_tn(grads, k_ref[keys, cols]) * SCALE

    squares(q_ref.shape[0], causal, flags_ref, square)
    if slope_q_ref is not None:
        gq_ref[...] = (sum_q_ref[...] * slope_q_ref[...].astype(F32)).astype(BF16)
    if slope_k_ref is not None:
        gk_ref[...] = (sum_k_ref[...] * slope_k_ref[...].astype(F32)).astype(BF16)


def backward(
    flags, q, k, v, grads, uq, uk, add_q=None, add_k=None, slope_q=None, slope_k=None, causal=False, after=()
):
    n, width = q.shape
    optional = [add_q, add_k, slope_q, slope_k]
    given = [x is not None for x in optional]
    args = [flags, q, k, v, grads, uq, uk] + [x for x in optional if x is not None]
    scratch = [] if slope_q is None else [pltpu.VMEM((n, width), F32)]
    scratch += [] if slope_k is None else [pltpu.VMEM((n, 2 * width), F32)]
    return call(
        functools.partial(backward_kernel, causal, given),
        [
            like(n, width, F32 if slope_q is None else BF16),
            like(n, 2 * width, F32 if slope_k is None else BF16),
        ],
        args,
        [SMEM] + [VMEM] * (len(args) - 1),
        scratch=scratch,
        flops=10 * n * n * width,
        nbytes=20 * n * width,
        name="backward",
        after=after,
    )


def gate_kernel(*refs):
    refs, (ga_ref, gated_ref, gu_ref) = refs[:-3], refs[-3:]
    own_ref, far_refs, (gg_ref, u_ref, slope_ref) = refs[0], refs[1:-3], refs[-3:]
    attended = own_ref[...]
    for far_ref in far_refs:
        attended = attended + far_ref[...].astype(F32)
    normed, inverse = centred(attended)
    gate = u_ref[...].astype(F32)
    grad = gg_ref[...]
    ga_ref[...] = back(normed, inverse, grad * gate).astype(BF16)
    gated_ref[...] = (normed * gate).astype(BF16)
    width = u_ref.shape[1]
    gu_ref[...] = (grad * normed * slope_ref[:, :width].astype(F32)).astype(BF16)


def product_kernel(x_ref, w_ref, out_ref):
    out_ref[...] = dot_nt(x_ref[...], w_ref[...]).astype(out_ref.dtype)


def output_kernel(gated_ref, w_ref, tokens_ref, out_ref):
    out_ref[...] = (dot(gated_ref[...], w_ref[...]) + tokens_ref[...].astype(F32)).astype(BF16)


def far_kernel(x_ref, wv_ref, wk_ref, out_ref):
    width = wv_ref.shape[1]
    out_ref[...] = (
        dot_nt(x_ref[:, :width], wv_ref[...]) + dot_nt(x_ref[:, width:], wk_ref[...])
    ).astype(out_ref.dtype)


def near_kernel(gu_ref, gvk_ref, gq_ref, wu_ref, wv_ref, wq_ref, wk_ref, *refs):
    width = wv_ref.shape[1]
    grad_q = gq_ref[...].astype(F32)
    for far_ref in refs[:-1]:
        grad_q = grad_q + far_ref[...].astype(F32)
    refs[-1][...] = (
        dot_nt(gu_ref[...], wu_ref[...])
        + dot_nt(gvk_ref[:, :width], wv_ref[...])
        + dot_nt(grad_q.astype(BF16), wq_ref[...])
        + dot_nt(gvk_ref[:, width:], wk_ref[...])
    )


def tokens_kernel(tokens_ref, cotangent_ref, near_ref, *refs):
    grad = near_ref[...]
    for far_ref in refs[:-1]:
        grad = grad + far_ref[...].astype(F32)
    scaled, inverse = centred(tokens_ref[...].astype(F32))
    refs[-1][...] = (back(scaled, inverse, grad) + cotangent_ref[...].astype(F32)).astype(BF16)


def orders(dp):
    bits = dp.bit_length() - 1
    return [0] + list(range(1, bits)), [0] + list(range(bits - 1, 0, -1))


def block_of(me, slot, dp):
    bits = dp.bit_length() - 1
    clear, set_ = [
        sum(((slot >> (bits - 1 - p)) & 1) << order[p] for p in range(bits)) for order in orders(dp)
    ]
    return me ^ jnp.where((me & 1) == (slot >> (bits - 1)), clear, set_)


def weight_kernel(dp, half, parts, me_ref, *refs):
    out_ref = refs[-1]
    n_slots, rows = out_ref.shape[0], out_ref.shape[1]
    blocks = [block_of(me_ref[0], s, dp) for s in range(half * n_slots, (half + 1) * n_slots)]
    taken, at = 0, 0
    for count, width in parts:
        total = None
        for _ in range(count):
            x_ref, g_ref = refs[taken], refs[taken + 1]
            taken += 2
            x = jnp.concatenate(
                [x_ref[:, pl.ds(pl.multiple_of(b * rows, rows), rows)] for b in blocks], axis=1
            )
            term = dot_tn(x, g_ref[...])
            total = term if total is None else total + term
        out_ref[:, :, at : at + width] = total.astype(BF16).reshape(n_slots, rows, width)
        at += width


def weight_half(me, parts, half, after=()):
    dp = lax.axis_size("dp")
    d = parts[0][0][0].shape[1]
    rows = d // dp
    widths = [pairs[0][1].shape[1] for pairs in parts]
    if rows % 128:
        total = jnp.concatenate(
            [sum(dot_tn(x, g) for x, g in pairs).astype(BF16) for pairs in parts], axis=1
        )
        return jnp.stack(
            [
                lax.dynamic_slice_in_dim(total, block_of(me[0], s, dp) * rows, rows)
                for s in range(half * dp // 2, (half + 1) * dp // 2)
            ]
        )
    args = [a for pairs in parts for pair in pairs for a in pair]
    n = args[0].shape[0]
    return call(
        functools.partial(weight_kernel, dp, half, [(len(p), w) for p, w in zip(parts, widths)]),
        jax.ShapeDtypeStruct((dp // 2, rows, sum(widths)), BF16),
        [me] + args,
        [SMEM] + [VMEM] * len(args),
        flops=sum(n * d * w * len(p) for p, w in zip(parts, widths)),
        nbytes=d * sum(widths),
        name="weights",
        after=after,
    )


def halve_kernel(mine_ref, other_ref, send_ref, keep_ref):
    half = send_ref.shape[0]
    total = mine_ref[...].astype(F32) + other_ref[...].astype(F32)
    send_ref[...] = total[half:].astype(BF16)
    keep_ref[...] = total[:half].astype(BF16)


def halve(mine, other, after=()):
    half = jax.ShapeDtypeStruct((mine.shape[0] // 2, *mine.shape[1:]), BF16)
    return call(halve_kernel, [half, half], [mine, other], name="halve", after=after)


def swap_dp(value, phase):
    dp = lax.axis_size("dp")
    pairs = [(i, i ^ (1 << orders(dp)[i & 1][phase])) for i in range(dp)]
    return lax.ppermute(value, "dp", pairs)


def over_seq(mine, other):
    n_seq, me = lax.axis_size("seq"), lax.axis_index("seq")
    rows, width = mine.shape[1] // n_seq, mine.shape[2]

    def chunk(index):
        start = (0, index * rows, 0)
        a = lax.dynamic_slice(mine, start, (1, rows, width))[0].astype(F32)
        return a + lax.dynamic_slice(other, start, (1, rows, width))[0].astype(F32)

    far = [
        lax.ppermute(chunk(me ^ r).astype(BF16), "seq", [(i, i ^ r) for i in range(n_seq)])
        for r in range(1, n_seq)
    ]
    return sum([value.astype(F32) for value in far], chunk(me))


def local(tokens_in, user_ids, w_in, w_out, cotangent):
    tokens, id_table, upstream = tokens_in[0], user_ids[0], cotangent[0]
    n, d = tokens.shape
    width = w_out.shape[0]
    n_seq = lax.axis_size("seq")
    span = n_seq // 2
    up = (span + 1) // 2
    down = span - up
    block = lax.axis_index("seq")
    me = lax.axis_index("dp").astype(jnp.int32).reshape(1)

    def users_of(index, missing):
        valid = (index >= 0) & (index < n_seq)
        ids = lax.dynamic_slice_in_dim(id_table, jnp.clip(index, 0, n_seq - 1) * n, n)
        return jnp.where(valid, ids, missing)

    def shared(later, earlier):
        step = n // 2
        return jnp.stack(
            [
                (later[c * step] == earlier[(e + 1) * step - 1]).astype(jnp.int32)
                for c in range(2)
                for e in range(2)
            ]
        )

    def col(ids):
        return ids.reshape(n, 1)

    def row(ids):
        return ids.reshape(1, n)

    far_tokens = [shift(tokens, by) for by in range(1, up + 1)]
    users = users_of(block, -1)
    next_users = users_of(block + up, -2)
    far_users = [users_of(block - by, -3) for by in range(1, up + 1)]
    no_flags = jnp.ones((4,), jnp.int32)

    normed, slope_q, query = project(tokens, w_in, [2], True)
    next_query = shift(query, -up) if down else None
    next_normed = shift(normed, -up) if down else None
    slope_u, gate, *_ = project(normed, w_in, [0], False)
    slope_vk, values, keys = project(normed, w_in, [1, 3], False, after=[gate])
    grad_gated = call(
        product_kernel, like(n, width, F32), [upstream, w_out], flops=2 * n * d * width,
        name="gated", after=[keys],
    )
    attended = forward(
        no_flags, query, keys, values, col(users), row(users), causal=True, after=[grad_gated]
    )

    pieces = []
    for by in range(1, up + 1):
        pieces.append(project(far_tokens[by - 1], w_in, [1, 3], True, after=[attended]))
    far_attended = []
    if down:
        partial = None
        for by in range(1, down + 1):
            _, _, far_values, far_keys = pieces[by - 1]
            partial = forward(
                shared(next_users, far_users[by - 1]), next_query, far_keys, far_values,
                col(next_users), row(far_users[by - 1]), partial, kind=BF16 if by == down else F32,
            )
        far_attended = [shift(partial, up)]
    for (_, _, far_values, far_keys), ids in zip(pieces, far_users):
        attended = forward(
            shared(users, ids), query, far_keys, far_values, col(users), row(ids), attended,
            after=[partial] if down else [],
        )
    ready = [attended]
    if down:
        next_slope, _ = project(next_normed, w_in, [2], False, after=[attended])
        ready = [next_slope]

    grad_attended, gated, grad_u = call(
        gate_kernel,
        [like(n, width, BF16)] * 3,
        [attended, *far_attended, grad_gated, gate, slope_u],
        name="gate",
        after=ready,
    )
    next_grad = shift(grad_attended, -up) if down else None
    early = [[(upstream, gated)], [(normed, grad_u)]]
    early_send = weight_half(me, early, 1)
    early_other = swap_dp(early_send, 0)
    early_mine = weight_half(me, early, 0, after=[early_send])

    grad_q, grad_vk = backward(
        no_flags, query, keys, values, grad_attended, row(users), col(users), slope_k=slope_vk,
        causal=True, after=[early_mine],
    )
    early_send, early_mine = halve(early_mine, early_other, after=[grad_vk])
    early_other = swap_dp(early_send, 1)
    far_sums = []
    for by, ((_, slope, far_values, far_keys), ids) in enumerate(zip(pieces, far_users), 1):
        grad_q, far_sum = backward(
            shared(users, ids), query, far_keys, far_values, grad_attended, row(users), col(ids),
            add_q=grad_q, slope_q=slope_q if by == up else None, slope_k=None if by <= down else slope,
            after=[early_send],
        )
        far_sums.append(far_sum)
    next_q = None
    for by in range(1, down + 1):
        _, slope, far_values, far_keys = pieces[by - 1]
        next_q, far_sums[by - 1] = backward(
            shared(next_users, far_users[by - 1]), next_query, far_keys, far_values, next_grad,
            row(next_users), col(far_users[by - 1]), add_q=next_q, add_k=far_sums[by - 1],
            slope_q=next_slope if by == down else None, slope_k=slope,
        )
    vk_pairs = [(normed, grad_vk)] + [(p[0], g) for p, g in zip(pieces, far_sums)]
    q_pairs = [(normed, grad_q)] + ([(next_normed, next_q)] if down else [])
    late = [vk_pairs, q_pairs]
    far_parts = []
    for by, grad in enumerate(far_sums, 1):
        part = call(
            far_kernel,
            like(n, d, BF16),
            [grad, w_in, w_in],
            [VMEM, columns(d, width, 1), columns(d, width, 3)],
            flops=4 * n * d * width,
            name="far",
        )
        far_parts.append(part)
    late_send = weight_half(me, late, 1, after=far_parts)
    far_parts = [shift(part, -by) for by, part in enumerate(far_parts, 1)]
    late_other = swap_dp(late_send, 0)
    late_mine = weight_half(me, late, 0, after=[late_send])
    next_q = [shift(next_q, up)] if down else []

    late_send, late_mine = halve(late_mine, late_other)
    late_other = swap_dp(late_send, 1)
    for phase in range(2, lax.axis_size("dp").bit_length() - 1):
        early_send, early_mine = halve(early_mine, early_other, after=[late_send])
        early_other = swap_dp(early_send, phase)
    output = call(
        output_kernel, like(n, d, BF16), [gated, w_out, tokens], flops=2 * n * d * width,
        name="output", after=[early_send],
    )
    early_sum = over_seq(early_mine, early_other)
    near = call(
        near_kernel,
        like(n, d, F32),
        [grad_u, grad_vk, grad_q] + [w_in] * 4 + next_q,
        [VMEM] * 3 + [columns(d, width, b) for b in range(4)] + [VMEM] * len(next_q),
        flops=8 * n * d * width,
        name="near",
        after=[output],
    )
    for phase in range(2, lax.axis_size("dp").bit_length() - 1):
        late_send, late_mine = halve(late_mine, late_other)
        late_other = swap_dp(late_send, phase)
    late_sum = over_seq(late_mine, late_other)
    grad_tokens = call(
        tokens_kernel, like(n, d, BF16), [tokens, upstream, near, *far_parts], name="tokens"
    )
    total_in = jnp.concatenate(
        [
            early_sum[:, width:],
            late_sum[:, :width],
            late_sum[:, 2 * width :],
            late_sum[:, width : 2 * width],
        ],
        axis=1,
    )
    return (output[None], grad_tokens[None], total_in, early_sum[:, :width].T)


def solution(mesh):
    in_specs = (P("dp", "seq", None), P("dp", None), P(), P(), P("dp", "seq", None))
    out_specs = (
        P("dp", "seq", None),
        P("dp", "seq", None),
        P(("dp", "seq"), None),
        P(None, ("dp", "seq")),
    )
    return jax.shard_map(local, mesh=mesh, in_specs=in_specs, out_specs=out_specs, check_vma=False)
```

```python
import functools
import math

import jax
import jax.numpy as jnp
from jax import lax
from jax.experimental import pallas as pl
from jax.experimental.pallas import tpu as pltpu
from jax.sharding import PartitionSpec as P

HEADS = 4
HD = 128
HALF_SCALE = 0.5 / math.sqrt(HD)
SCALE = 1.0 / math.sqrt(HD)
EPSILON = 1e-05
GRANT = 18 << 20
BF16 = jnp.bfloat16
F32 = jnp.float32
VMEM = pl.BlockSpec(memory_space=pltpu.VMEM)
SMEM = pl.BlockSpec(memory_space=pltpu.SMEM)


def shift(value, by):
    devices = lax.axis_size("seq")
    pairs = [(i, i + by) for i in range(devices) if 0 <= i + by < devices]
    return lax.ppermute(value, "seq", pairs)


def call(kernel, outs, args, specs=None, scratch=(), flops=0, nbytes=0, name=None, after=(), weight=8):
    first, last = len(args), len(args) + len(after)

    def body(*refs):
        kernel(*refs[:first], *refs[last:])

    return pl.pallas_call(
        body,
        grid=(1,),
        out_shape=outs,
        in_specs=(specs or [VMEM] * first) + [pl.BlockSpec(memory_space=pl.ANY)] * len(after),
        out_specs=jax.tree.map(lambda _: VMEM, outs),
        scratch_shapes=scratch,
        compiler_params=pltpu.CompilerParams(vmem_limit_bytes=GRANT),
        cost_estimate=pl.CostEstimate(
            flops=weight * flops, bytes_accessed=nbytes, transcendentals=0
        ),
        name=name,
    )(*args, *after)


def columns(rows, width, block):
    return pl.BlockSpec((rows, width), lambda i: (0, block))


def like(rows, width, kind):
    return jax.ShapeDtypeStruct((rows, width), kind)


def dot(a, b):
    return jnp.dot(a, b, preferred_element_type=F32)


def dot_nt(a, b):
    return lax.dot_general(a, b, (((1,), (1,)), ((), ())), preferred_element_type=F32)


def dot_tn(a, b):
    return lax.dot_general(a, b, (((0,), (0,)), ((), ())), preferred_element_type=F32)


def centred(values):
    center = values - jnp.mean(values, axis=-1, keepdims=True)
    inverse = lax.rsqrt(jnp.mean(center * center, axis=-1, keepdims=True) + EPSILON)
    return center * inverse, inverse


def back(scaled, inverse, upstream):
    return inverse * (
        upstream
        - jnp.mean(upstream, axis=-1, keepdims=True)
        - scaled * jnp.mean(upstream * scaled, axis=-1, keepdims=True)
    )


def silu_and_slope(half):
    bend = 1.0 + jnp.tanh(half)
    value = half * bend
    return value, 0.5 * (bend + value * (2.0 - bend))


def project_kernel(raw, blocks, x_ref, *refs):
    w_refs, refs = refs[:blocks], refs[blocks:]
    if raw == "send":
        refs, (normed_send, act_send) = refs[:-2], refs[-2:]
    if raw:
        normed_ref, refs = refs[0], refs[1:]
        normed_ref[...] = centred(x_ref[...].astype(F32))[0].astype(BF16)
    else:
        normed_ref = x_ref
    slope_ref, act_refs = refs[0], refs[1:]
    width = slope_ref.shape[1] // blocks
    for b in range(blocks):
        value, slope = silu_and_slope(0.5 * dot(normed_ref[...], w_refs[b][...]))
        act_refs[b][...] = value.astype(BF16)
        slope_ref[:, b * width : (b + 1) * width] = slope.astype(BF16)
    if raw == "send":
        normed_send[...] = normed_ref[...]
        act_send[...] = act_refs[0][...]


def project(x, w_in, blocks, raw, after=()):
    n, d = x.shape
    width = w_in.shape[1] // 4
    outs = [like(n, d, BF16)] if raw else []
    outs += [like(n, width * len(blocks), BF16)] + [like(n, width, BF16)] * len(blocks)
    outs += [like(n, d, BF16), like(n, width, BF16)] if raw == "send" else []
    return call(
        functools.partial(project_kernel, raw, len(blocks)),
        outs,
        [x] + [w_in] * len(blocks),
        [VMEM] + [columns(d, width, b) for b in blocks],
        flops=2 * n * d * width * len(blocks),
        nbytes=2 * n * d + 2 * d * width * len(blocks),
        name="project",
        after=after,
    )


def pair_loop(kind, chunks, later, earlier, place_ref, ids_ref, n, n_seq, body):
    step = n // 2
    if kind == "own":
        for c in reversed(chunks):
            rows = c * step
            body(slice(rows, rows + step), slice(0, rows + step), rows, c == chunks[-1])
        return
    q_block, k_block = place_ref[1] + later, place_ref[1] - earlier
    valid = (q_block < n_seq) & (k_block >= 0)
    q_start, k_start = jnp.minimum(q_block, n_seq - 1) * n, jnp.maximum(k_block, 0) * n
    crosses = valid & (ids_ref[0, q_start + chunks[0] * step] == ids_ref[0, k_start + n - 1])
    if kind == "near":
        rows = slice(chunks[0] * step, (chunks[-1] + 1) * step)
        pl.when(crosses)(lambda: body(rows, slice(0, n), None, False))
        return

    @pl.loop(0, 2 * len(chunks))
    def _(i):
        row = pl.multiple_of((chunks[0] + i // 2) * step, step)
        key = pl.multiple_of((i % 2) * step, step)
        shared = ids_ref[0, q_start + row] == ids_ref[0, k_start + key + step - 1]
        pl.when(valid & shared)(
            lambda: body(pl.ds(row, step), pl.ds(key, step), None, False)
        )


def extent(part):
    if isinstance(part, slice):
        return part.start, part.stop - part.start
    return part.start, part.size


def ids_of(ref, block, rows, n, n_seq, axis):
    first, size = extent(rows)
    start = pl.multiple_of(jnp.clip(block, 0, n_seq - 1) * n, n) + first
    start = pl.multiple_of(start, size) if not isinstance(first, int) else start
    return ref[pl.ds(start, size), :] if axis == 0 else ref[:, pl.ds(start, size)]


def forward_kernel(
    n_seq, kind, chunks, later, earlier, more, place_ref, ids_ref, row_ref, col_ref, q_ref, k_ref, v_ref, *refs
):
    refs = list(refs)
    add_ref = refs.pop(0) if more else None
    out_ref = refs.pop(0)
    if kind != "far":
        refs.pop(0)[...] = k_ref[...].T
    sum_ref = refs.pop(0) if refs else out_ref
    n = q_ref.shape[0]
    base = chunks[0] * (n // 2)
    me = place_ref[1]
    if more or kind != "own":
        sum_ref[...] = add_ref[...] if more else jnp.zeros_like(sum_ref)

    def part(rows, keys, offset, first):
        first_row, size = extent(rows)
        out = slice(first_row - base, first_row - base + size) if kind != "far" else slice(0, size)
        mask = ids_of(col_ref, me + later, rows, n, n_seq, 0) == ids_of(row_ref, me - earlier, keys, n, n_seq, 1)
        if offset is not None:
            mask &= lax.broadcasted_iota(jnp.int32, mask.shape, 1) <= offset + lax.broadcasted_iota(
                jnp.int32, mask.shape, 0
            )
        for h in range(HEADS):
            cols = slice(h * HD, (h + 1) * HD)
            half = dot_nt(q_ref[rows, cols], k_ref[keys, cols]) * HALF_SCALE
            weights = jnp.where(mask, half * (1.0 + jnp.tanh(half)), 0.0).astype(BF16)
            term = dot(weights, v_ref[keys, cols])
            sum_ref[out, cols] = term if kind == "own" and not more else sum_ref[out, cols] + term

    pair_loop(kind, chunks, later, earlier, place_ref, ids_ref, n, n_seq, part)
    if sum_ref is not out_ref:
        out_ref[...] = sum_ref[...].astype(out_ref.dtype)


def forward(users, kind, q, k, v, later=0, earlier=0, add=None, dtype=F32, chunks=(0, 1), after=()):
    n, width = q.shape
    args = [*users, q, k, v] + ([] if add is None else [add])
    return call(
        functools.partial(
            forward_kernel, lax.axis_size("seq"), kind, chunks, later, earlier, add is not None
        ),
        [like(n // 2 * len(chunks), width, dtype)] + ([] if kind == "far" else [like(width, n, BF16)]),
        args,
        [SMEM] * 2 + [VMEM] * (len(args) - 2),
        scratch=[] if dtype == F32 else [pltpu.VMEM((n // 2 * len(chunks), width), F32)],
        flops=2 * n * n * width * len(chunks),
        nbytes=10 * n * width,
        name="forward",
        after=after,
    )


def backward_kernel(
    n_seq, kind, chunks, later, earlier, halves, given, place_ref, ids_ref, row_ref, col_ref, q_ref, k_ref, kt_ref, v_ref, *refs
):
    refs = list(refs)
    g_refs = [refs.pop(0) for _ in range(max(halves, 1))]
    add_q_ref, add_k_ref, slope_q_ref, slope_k_ref = [refs.pop(0) if x else None for x in given]
    gq_ref, gk_ref = refs.pop(0), refs.pop(0)
    sum_q_ref = gq_ref if slope_q_ref is None else refs.pop(0)
    sum_k_ref = gk_ref if slope_k_ref is None else refs.pop(0)
    n, width = q_ref.shape
    g_ref = g_refs[0]
    if halves == 2:
        g_ref = refs.pop(0)
        g_ref[: n // 2, :] = g_refs[0][...]
        g_ref[n // 2 :, :] = g_refs[1][...]
    me = place_ref[1]
    added = 0 if add_q_ref is None else add_q_ref.shape[0]
    if added:
        sum_q_ref[:added, :] = add_q_ref[...]
    if added < sum_q_ref.shape[0]:
        sum_q_ref[added:, :] = jnp.zeros_like(sum_q_ref[added:, :])
    if kind != "own":
        sum_k_ref[...] = jnp.zeros_like(sum_k_ref) if add_k_ref is None else add_k_ref[...]

    def part(rows, keys, offset, first):
        mask = ids_of(col_ref, me - earlier, keys, n, n_seq, 0) == ids_of(row_ref, me + later, rows, n, n_seq, 1)
        if offset is not None:
            mask &= lax.broadcasted_iota(jnp.int32, mask.shape, 0) <= offset + lax.broadcasted_iota(
                jnp.int32, mask.shape, 1
            )
        for h in range(HEADS):
            cols = slice(h * HD, (h + 1) * HD)
            k_cols = slice(width + h * HD, width + (h + 1) * HD)
            g = g_ref[rows, cols]
            half = dot_nt(k_ref[keys, cols], q_ref[rows, cols]) * HALF_SCALE
            bend = jnp.where(mask, 1.0 + jnp.tanh(half), 0.0)
            value = half * bend
            weights = value.astype(BF16)
            grads = (dot_nt(v_ref[keys, cols], g) * (bend + value * (2.0 - bend))).astype(BF16)
            part_v = dot(weights, g)
            part_k = dot(grads, q_ref[rows, cols]) * HALF_SCALE
            part_q = dot(kt_ref[cols, keys], grads).T * HALF_SCALE
            sum_k_ref[keys, cols] = part_v if first else sum_k_ref[keys, cols] + part_v
            sum_k_ref[keys, k_cols] = part_k if first else sum_k_ref[keys, k_cols] + part_k
            sum_q_ref[rows, cols] += part_q

    pair_loop(kind, chunks, later, earlier, place_ref, ids_ref, n, n_seq, part)
    if slope_q_ref is not None:
        gq_ref[...] = (sum_q_ref[...] * slope_q_ref[...].astype(F32)).astype(BF16)
    if slope_k_ref is not None:
        gk_ref[...] = (sum_k_ref[...] * slope_k_ref[...].astype(F32)).astype(BF16)


def backward(
    users, kind, q, keys, v, grads, later=0, earlier=0, add_q=None, add_k=None, slope_q=None, slope_k=None,
    chunks=(0, 1), after=()
):
    n, width = q.shape
    halves = len(grads) if isinstance(grads, list) else 0
    optional = [add_q, add_k, slope_q, slope_k]
    given = [x is not None for x in optional]
    args = [*users, q, *keys, v, *(grads if halves else [grads])] + [x for x in optional if x is not None]
    q_rows = n if 1 in chunks else n // 2
    scratch = [] if slope_q is None else [pltpu.VMEM((q_rows, width), F32)]
    scratch += [] if slope_k is None else [pltpu.VMEM((n, 2 * width), F32)]
    scratch += [pltpu.VMEM((n, width), BF16)] if halves == 2 else []
    return call(
        functools.partial(
            backward_kernel, lax.axis_size("seq"), kind, chunks, later, earlier, halves, given
        ),
        [
            like(q_rows, width, F32 if slope_q is None else BF16),
            like(n, 2 * width, F32 if slope_k is None else BF16),
        ],
        args,
        [SMEM] * 2 + [VMEM] * (len(args) - 2),
        scratch=scratch,
        flops=5 * n * n * width * len(chunks),
        nbytes=20 * n * width,
        name="backward",
        after=after,
    )


def gate_kernel(start, far, *refs):
    refs = list(refs)
    far_refs = [refs.pop(0) for _ in range(far)]
    own_ref, gg_ref, u_ref, slope_ref = refs[:4]
    outs = refs[-3:] if start == 0 else refs[-4:-1]
    n = far_refs[0].shape[0] if far_refs else own_ref.shape[0]
    rows = slice(start, start + n)
    attended = own_ref[rows, :]
    for far_ref in far_refs:
        attended = attended + far_ref[...].astype(F32)
    normed, inverse = centred(attended)
    gate = u_ref[rows, :].astype(F32)
    grad = gg_ref[rows, :]
    width = u_ref.shape[1]
    grad_attended = back(normed, inverse, grad * gate).astype(BF16)
    results = [
        grad_attended,
        (normed * gate).astype(BF16),
        (grad * normed * slope_ref[rows, :width].astype(F32)).astype(BF16),
    ]
    for out, result in zip(outs, results):
        out[rows, :] = result
    if start:
        refs[-1][...] = grad_attended
        for out, before in zip(outs, refs[4:7]):
            out[:start, :] = before[...]


def product_kernel(x_ref, w_ref, out_ref):
    out_ref[...] = dot_nt(x_ref[...], w_ref[...]).astype(out_ref.dtype)


def output_kernel(gated_ref, w_ref, tokens_ref, out_ref):
    out_ref[...] = (dot(gated_ref[...], w_ref[...]) + tokens_ref[...].astype(F32)).astype(BF16)


def far_kernel(x_ref, wv_ref, wk_ref, out_ref):
    width = wv_ref.shape[1]
    out_ref[...] = (
        dot_nt(x_ref[:, :width], wv_ref[...]) + dot_nt(x_ref[:, width:], wk_ref[...])
    ).astype(out_ref.dtype)


def near_kernel(gu_ref, gvk_ref, gq_ref, wu_ref, wv_ref, wq_ref, wk_ref, *refs):
    width = wv_ref.shape[1]
    grad_q = gq_ref[...].astype(F32)
    for far_ref in refs[:-1]:
        grad_q = grad_q + far_ref[...].astype(F32)
    refs[-1][...] = (
        dot_nt(gu_ref[...], wu_ref[...])
        + dot_nt(gvk_ref[:, :width], wv_ref[...])
        + dot_nt(grad_q.astype(BF16), wq_ref[...])
        + dot_nt(gvk_ref[:, width:], wk_ref[...])
    )


def tokens_kernel(tokens_ref, cotangent_ref, near_ref, *refs):
    grad = near_ref[...]
    for far_ref in refs[:-1]:
        grad = grad + far_ref[...].astype(F32)
    scaled, inverse = centred(tokens_ref[...].astype(F32))
    refs[-1][...] = (back(scaled, inverse, grad) + cotangent_ref[...].astype(F32)).astype(BF16)


def orders(dp):
    bits = dp.bit_length() - 1
    return [0] + list(range(1, bits)), [0] + list(range(bits - 1, 0, -1))


def block_of(me, slot, dp):
    bits = dp.bit_length() - 1
    clear, set_ = [
        sum(((slot >> (bits - 1 - p)) & 1) << order[p] for p in range(bits)) for order in orders(dp)
    ]
    return me ^ jnp.where((me & 1) == (slot >> (bits - 1)), clear, set_)


def weight_kernel(dp, half, parts, place_ref, *refs):
    out_ref = refs[-1]
    n_slots, rows = out_ref.shape[0], out_ref.shape[1]
    blocks = [block_of(place_ref[0], s, dp) for s in range(half * n_slots, (half + 1) * n_slots)]
    taken, at = 0, 0
    for count, width in parts:
        total = None
        for _ in range(count):
            x_ref, g_ref = refs[taken], refs[taken + 1]
            taken += 2
            x = jnp.concatenate(
                [x_ref[:, pl.ds(pl.multiple_of(b * rows, rows), rows)] for b in blocks], axis=1
            )
            term = dot_tn(x, g_ref[...])
            total = term if total is None else total + term
        out_ref[:, :, at : at + width] = total.astype(BF16).reshape(n_slots, rows, width)
        at += width


def weight_half(place, parts, half, after=(), weight=8):
    dp = lax.axis_size("dp")
    d = parts[0][0][0].shape[1]
    rows = d // dp
    widths = [pairs[0][1].shape[1] for pairs in parts]
    if rows % 128:
        total = jnp.concatenate(
            [sum(dot_tn(x, g) for x, g in pairs).astype(BF16) for pairs in parts], axis=1
        )
        return jnp.stack(
            [
                lax.dynamic_slice_in_dim(total, block_of(place[0], s, dp) * rows, rows)
                for s in range(half * dp // 2, (half + 1) * dp // 2)
            ]
        )
    args = [a for pairs in parts for pair in pairs for a in pair]
    n = args[0].shape[0]
    return call(
        functools.partial(weight_kernel, dp, half, [(len(p), w) for p, w in zip(parts, widths)]),
        jax.ShapeDtypeStruct((dp // 2, rows, sum(widths)), BF16),
        [place] + args,
        [SMEM] + [VMEM] * len(args),
        flops=sum(n * d * w * len(p) for p, w in zip(parts, widths)),
        nbytes=d * sum(widths),
        name="weights",
        after=after,
        weight=weight,
    )


def halve_kernel(mine_ref, other_ref, send_ref, keep_ref):
    half = send_ref.shape[0]
    total = mine_ref[...].astype(F32) + other_ref[...].astype(F32)
    send_ref[...] = total[half:].astype(BF16)
    keep_ref[...] = total[:half].astype(BF16)


def halve(mine, other, after=()):
    half = jax.ShapeDtypeStruct((mine.shape[0] // 2, *mine.shape[1:]), BF16)
    return call(halve_kernel, [half, half], [mine, other], name="halve", after=after)


def swap_dp(value, phase):
    dp = lax.axis_size("dp")
    pairs = [(i, i ^ (1 << orders(dp)[i & 1][phase])) for i in range(dp)]
    return lax.ppermute(value, "dp", pairs)


def over_seq(mine, other):
    n_seq, me = lax.axis_size("seq"), lax.axis_index("seq")
    rows, width = mine.shape[1] // n_seq, mine.shape[2]

    def chunk(index):
        start = (0, index * rows, 0)
        a = lax.dynamic_slice(mine, start, (1, rows, width))[0].astype(F32)
        return a + lax.dynamic_slice(other, start, (1, rows, width))[0].astype(F32)

    far = [
        lax.ppermute(chunk(me ^ r).astype(BF16), "seq", [(i, i ^ r) for i in range(n_seq)])
        for r in range(1, n_seq)
    ]
    return [chunk(me), *far]


def total_kernel(*refs):
    in_ref, out_ref = refs[-2:]
    count = (len(refs) - 2) // 2
    early, late = [
        sum([ref[...].astype(F32) for ref in part[1:]], part[0][...])
        for part in (refs[:count], refs[count : 2 * count])
    ]
    width = in_ref.shape[1] // 4
    in_ref[:, :width] = early[:, width:]
    in_ref[:, width : 2 * width] = late[:, :width]
    in_ref[:, 2 * width : 3 * width] = late[:, 2 * width :]
    in_ref[:, 3 * width :] = late[:, width : 2 * width]
    out_ref[...] = early[:, :width]


def local(tokens_in, user_ids, w_in, w_out, cotangent):
    tokens, id_table, upstream = tokens_in[0], user_ids[0], cotangent[0]
    n, d = tokens.shape
    width = w_out.shape[0]
    n_seq = lax.axis_size("seq")
    span = n_seq // 2
    up = (span + 1) // 2
    down = span - up
    place = jnp.stack([lax.axis_index("dp"), lax.axis_index("seq")]).astype(jnp.int32)
    ids = id_table.reshape(1, -1)
    users = [place, ids, ids, id_table.reshape(-1, 1)]

    far_tokens = [shift(tokens, by) for by in range(1, up + 1)]
    normed, slope_q, query, *sent = project(tokens, w_in, [2], "send" if down else True)
    if down:
        next_normed, next_query = [shift(x, -up) for x in sent]
    slope_u, gate, *_ = project(normed, w_in, [0], False)
    slope_vk, values, keys = project(normed, w_in, [1, 3], False, after=[gate])
    grad_gated = call(
        product_kernel, like(n, width, F32), [upstream, w_out], flops=2 * n * d * width,
        name="gated", after=[keys],
    )
    attended, keys_t = forward(users, "own", query, keys, values, after=[grad_gated])

    pieces = []
    for by in range(1, up + 1):
        pieces.append(project(far_tokens[by - 1], w_in, [1, 3], True, after=[attended]))
    far_attended = []
    order = [attended]
    if down:
        for half in (0, 1):
            partial = None
            for by in range(1, down + 1):
                _, _, far_values, far_keys = pieces[by - 1]
                [partial] = forward(
                    users, "far", next_query, far_keys, far_values, up, by, partial,
                    BF16 if by == down else F32, (half,), order,
                )
            order = [partial]
            far_attended.append(shift(partial, up))
    for by, (far_normed, slope, far_values, far_keys) in enumerate(pieces, 1):
        attended, far_t = forward(
            users, "near", query, far_keys, far_values, 0, by, attended, after=order
        )
        pieces[by - 1] = (far_normed, slope, far_values, (far_keys, far_t))

    gate_args = [attended, grad_gated, gate, slope_u]
    far_sums = [None] * up
    if down:
        first = call(
            functools.partial(gate_kernel, 0, 1),
            [like(n // 2, width, BF16)] * 3,
            [far_attended[0], *gate_args],
            flops=500 * n * width,
            name="gate",
        )
        next_grad = [shift(first[0], -up)]
        grad_q = None
        for by, (_, _, far_values, far_keys) in enumerate(pieces, 1):
            grad_q, far_sums[by - 1] = backward(
                users, "near", query, far_keys, far_values, [first[0]], 0, by, add_q=grad_q, chunks=(0,)
            )
        grad_attended, gated, grad_u, second = call(
            functools.partial(gate_kernel, n // 2, 1),
            [like(n, width, BF16)] * 3 + [like(n // 2, width, BF16)],
            [far_attended[1], *gate_args, *first],
            flops=500 * n * width,
            name="gate",
            after=[grad_q],
        )
        next_grad.append(shift(second, -up))
        rest = (1,)
    else:
        grad_attended, gated, grad_u = call(
            functools.partial(gate_kernel, 0, 0), [like(n, width, BF16)] * 3, gate_args, name="gate"
        )
        grad_q, rest = None, (0, 1)
    early = [[(upstream, gated)], [(normed, grad_u)]]
    early_send = weight_half(place, early, 1)
    early_other = swap_dp(early_send, 0)
    grad_q, grad_vk = backward(
        users, "own", query, (keys, keys_t), values, grad_attended, add_q=grad_q, slope_k=slope_vk,
        after=[early_send] + ([next_normed] if down else []),
    )
    early_mine = weight_half(place, early, 0, after=[grad_vk])
    early_send, early_mine = halve(early_mine, early_other)
    early_other = swap_dp(early_send, 1)
    for by, (_, slope, far_values, far_keys) in enumerate(pieces, 1):
        grad_q, far_sums[by - 1] = backward(
            users, "near", query, far_keys, far_values, grad_attended, 0, by, add_q=grad_q,
            add_k=far_sums[by - 1], slope_q=slope_q if by == up else None,
            slope_k=None if by <= down else slope, chunks=rest, after=[early_send],
        )
    if down:
        next_slope, _ = project(next_normed, w_in, [2], False, after=[grad_q])
    next_q = None
    for by in range(1, down + 1):
        _, slope, far_values, far_keys = pieces[by - 1]
        next_q, far_sums[by - 1] = backward(
            users, "far", next_query, far_keys, far_values, next_grad, up, by,
            add_q=next_q, add_k=far_sums[by - 1],
            slope_q=next_slope if by == down else None, slope_k=slope,
        )
    vk_pairs = [(normed, grad_vk)] + [(p[0], g) for p, g in zip(pieces, far_sums)]
    q_pairs = [(normed, grad_q)] + ([(next_normed, next_q)] if down else [])
    late = [vk_pairs, q_pairs]
    phases = range(2, lax.axis_size("dp").bit_length() - 1)
    order = [next_q] if down else [grad_q]
    for phase in phases:
        early_send, early_mine = halve(early_mine, early_other, after=order)
        early_other = swap_dp(early_send, phase)
        order = [early_send]
    late_send = weight_half(place, late, 1, after=order, weight=1)
    late_other = swap_dp(late_send, 0)
    late_mine = weight_half(place, late, 0, after=[late_send], weight=1)
    late_send, late_mine = halve(late_mine, late_other)
    late_other = swap_dp(late_send, 1)
    far_parts = []
    for by, grad in enumerate(far_sums, 1):
        part = call(
            far_kernel,
            like(n, d, BF16),
            [grad, w_in, w_in],
            [VMEM, columns(d, width, 1), columns(d, width, 3)],
            flops=4 * n * d * width,
            name="far", weight=1,
            after=[late_send],
        )
        far_parts.append(part)
    order = far_parts
    far_parts = [shift(part, -by) for by, part in enumerate(far_parts, 1)]
    next_q = [shift(next_q, up)] if down else []
    output = call(
        output_kernel, like(n, d, BF16), [gated, w_out, tokens], flops=2 * n * d * width,
        name="output", weight=0, after=[*order, early_other, *next_q],
    )
    early_sum = over_seq(early_mine, early_other)
    order = [output]
    for phase in phases:
        late_send, late_mine = halve(late_mine, late_other, after=order)
        late_other = swap_dp(late_send, phase)
        order = [late_send]
    late_sum = over_seq(late_mine, late_other)
    near = call(
        near_kernel,
        like(n, d, F32),
        [grad_u, grad_vk, grad_q] + [w_in] * 4 + next_q,
        [VMEM] * 3 + [columns(d, width, b) for b in range(4)] + [VMEM] * len(next_q),
        flops=8 * n * d * width,
        name="near", weight=0,
        after=[*order, late_other],
    )
    grad_tokens = call(
        tokens_kernel, like(n, d, BF16), [tokens, upstream, near, *far_parts], name="tokens", weight=0,
        after=[late_other],
    )
    rows = early_sum[0].shape[0]
    total_in, out_w = call(
        total_kernel,
        [like(rows, 4 * width, F32), like(rows, width, F32)],
        [*early_sum, *late_sum],
        name="total",
        after=[grad_tokens],
    )
    return (output[None], grad_tokens[None], total_in, out_w.T)


def solution(mesh):
    in_specs = (P("dp", "seq", None), P("dp", None), P(), P(), P("dp", "seq", None))
    out_specs = (
        P("dp", "seq", None),
        P("dp", "seq", None),
        P(("dp", "seq"), None),
        P(None, ("dp", "seq")),
    )
    return jax.shard_map(local, mesh=mesh, in_specs=in_specs, out_specs=out_specs, check_vma=False)
```

```python
import functools
import math

import jax
import jax.numpy as jnp
from jax import lax
from jax.experimental import pallas as pl
from jax.experimental.pallas import tpu as pltpu
from jax.sharding import PartitionSpec as P

HEADS = 4
HD = 128
HALF_SCALE = 0.5 / math.sqrt(HD)
SCALE = 1.0 / math.sqrt(HD)
EPSILON = 1e-05
GRANT = 18 << 20
BF16 = jnp.bfloat16
F32 = jnp.float32
VMEM = pl.BlockSpec(memory_space=pltpu.VMEM)
SMEM = pl.BlockSpec(memory_space=pltpu.SMEM)


def shift(value, by):
    devices = lax.axis_size("seq")
    pairs = [(i, i + by) for i in range(devices) if 0 <= i + by < devices]
    return lax.ppermute(value, "seq", pairs)


def call(
    kernel, outs, args, specs=None, scratch=(), flops=0, nbytes=0, name=None, after=(), weight=8, out_specs=None
):
    first, last = len(args), len(args) + len(after)

    def body(*refs):
        kernel(*refs[:first], *refs[last:])

    return pl.pallas_call(
        body,
        grid=(1,),
        out_shape=outs,
        in_specs=(specs or [VMEM] * first) + [pl.BlockSpec(memory_space=pl.ANY)] * len(after),
        out_specs=out_specs or jax.tree.map(lambda _: VMEM, outs),
        scratch_shapes=scratch,
        compiler_params=pltpu.CompilerParams(vmem_limit_bytes=GRANT),
        cost_estimate=pl.CostEstimate(
            flops=weight * flops, bytes_accessed=nbytes, transcendentals=0
        ),
        name=name,
    )(*args, *after)


def columns(rows, width, block):
    return pl.BlockSpec((rows, width), lambda i: (0, block))


def like(rows, width, kind):
    return jax.ShapeDtypeStruct((rows, width), kind)


def dot(a, b):
    return jnp.dot(a, b, preferred_element_type=F32)


def dot_nt(a, b):
    return lax.dot_general(a, b, (((1,), (1,)), ((), ())), preferred_element_type=F32)


def dot_tn(a, b):
    return lax.dot_general(a, b, (((0,), (0,)), ((), ())), preferred_element_type=F32)


def centred(values):
    center = values - jnp.mean(values, axis=-1, keepdims=True)
    inverse = lax.rsqrt(jnp.mean(center * center, axis=-1, keepdims=True) + EPSILON)
    return center * inverse, inverse


def back(scaled, inverse, upstream):
    return inverse * (
        upstream
        - jnp.mean(upstream, axis=-1, keepdims=True)
        - scaled * jnp.mean(upstream * scaled, axis=-1, keepdims=True)
    )


def silu_and_slope(half):
    bend = 1.0 + jnp.tanh(half)
    value = half * bend
    return value, 0.5 * (bend + value * (2.0 - bend))


def project_kernel(raw, blocks, x_ref, *refs):
    w_refs, refs = refs[:blocks], refs[blocks:]
    if raw == "send":
        refs, (normed_send, act_send) = refs[:-2], refs[-2:]
    if raw:
        normed_ref, refs = refs[0], refs[1:]
        normed_ref[...] = centred(x_ref[...].astype(F32))[0].astype(BF16)
    else:
        normed_ref = x_ref
    slope_ref, act_refs = refs[0], refs[1:]
    width = slope_ref.shape[1] // blocks
    for b in range(blocks):
        value, slope = silu_and_slope(0.5 * dot(normed_ref[...], w_refs[b][...]))
        act_refs[b][...] = value.astype(BF16)
        slope_ref[:, b * width : (b + 1) * width] = slope.astype(BF16)
    if raw == "send":
        normed_send[...] = normed_ref[...]
        act_send[...] = act_refs[0][...]


def project(x, w_in, blocks, raw, after=()):
    n, d = x.shape
    width = w_in.shape[1] // 4
    outs = [like(n, d, BF16)] if raw else []
    outs += [like(n, width * len(blocks), BF16)] + [like(n, width, BF16)] * len(blocks)
    outs += [like(n, d, BF16), like(n, width, BF16)] if raw == "send" else []
    return call(
        functools.partial(project_kernel, raw, len(blocks)),
        outs,
        [x] + [w_in] * len(blocks),
        [VMEM] + [columns(d, width, b) for b in blocks],
        flops=2 * n * d * width * len(blocks),
        nbytes=2 * n * d + 2 * d * width * len(blocks),
        name="project",
        after=after,
    )


def pair_loop(kind, chunks, later, earlier, place_ref, ids_ref, n, n_seq, body):
    step = n // 2
    if kind == "own":
        for c in reversed(chunks):
            rows = c * step
            body(slice(rows, rows + step), slice(0, rows + step), rows, c == chunks[-1])
        return
    q_block, k_block = place_ref[1] + later, place_ref[1] - earlier
    valid = (q_block < n_seq) & (k_block >= 0)
    q_start, k_start = jnp.minimum(q_block, n_seq - 1) * n, jnp.maximum(k_block, 0) * n
    crosses = valid & (ids_ref[0, q_start + chunks[0] * step] == ids_ref[0, k_start + n - 1])
    if kind == "near":
        rows = slice(chunks[0] * step, (chunks[-1] + 1) * step)
        pl.when(crosses)(lambda: body(rows, slice(0, n), None, False))
        return

    @pl.loop(0, 2 * len(chunks))
    def _(i):
        row = pl.multiple_of((chunks[0] + i // 2) * step, step)
        key = pl.multiple_of((i % 2) * step, step)
        shared = ids_ref[0, q_start + row] == ids_ref[0, k_start + key + step - 1]
        pl.when(valid & shared)(
            lambda: body(pl.ds(row, step), pl.ds(key, step), None, False)
        )


def extent(part):
    if isinstance(part, slice):
        return part.start, part.stop - part.start
    return part.start, part.size


def ids_of(ref, block, rows, n, n_seq, axis):
    first, size = extent(rows)
    start = pl.multiple_of(jnp.clip(block, 0, n_seq - 1) * n, n) + first
    start = pl.multiple_of(start, size) if not isinstance(first, int) else start
    return ref[pl.ds(start, size), :] if axis == 0 else ref[:, pl.ds(start, size)]


def forward_kernel(
    n_seq, kind, chunks, later, earlier, more, place_ref, ids_ref, row_ref, col_ref, q_ref, k_ref, v_ref, *refs
):
    refs = list(refs)
    add_ref = refs.pop(0) if more else None
    out_ref = refs.pop(0)
    if kind != "far":
        refs.pop(0)[...] = k_ref[...].T
    sum_ref = refs.pop(0) if refs else out_ref
    n = q_ref.shape[0]
    base = chunks[0] * (n // 2)
    me = place_ref[1]
    if more or kind != "own":
        sum_ref[...] = add_ref[...] if more else jnp.zeros_like(sum_ref)

    def part(rows, keys, offset, first):
        first_row, size = extent(rows)
        out = slice(first_row - base, first_row - base + size) if kind != "far" else slice(0, size)
        mask = ids_of(col_ref, me + later, rows, n, n_seq, 0) == ids_of(row_ref, me - earlier, keys, n, n_seq, 1)
        if offset is not None:
            mask &= lax.broadcasted_iota(jnp.int32, mask.shape, 1) <= offset + lax.broadcasted_iota(
                jnp.int32, mask.shape, 0
            )
        for h in range(HEADS):
            cols = slice(h * HD, (h + 1) * HD)
            half = dot_nt(q_ref[rows, cols], k_ref[keys, cols]) * HALF_SCALE
            weights = jnp.where(mask, half * (1.0 + jnp.tanh(half)), 0.0).astype(BF16)
            term = dot(weights, v_ref[keys, cols])
            sum_ref[out, cols] = term if kind == "own" and not more else sum_ref[out, cols] + term

    pair_loop(kind, chunks, later, earlier, place_ref, ids_ref, n, n_seq, part)
    if sum_ref is not out_ref:
        out_ref[...] = sum_ref[...].astype(out_ref.dtype)


def forward(users, kind, q, k, v, later=0, earlier=0, add=None, dtype=F32, chunks=(0, 1), after=()):
    n, width = q.shape
    args = [*users, q, k, v] + ([] if add is None else [add])
    return call(
        functools.partial(
            forward_kernel, lax.axis_size("seq"), kind, chunks, later, earlier, add is not None
        ),
        [like(n // 2 * len(chunks), width, dtype)] + ([] if kind == "far" else [like(width, n, BF16)]),
        args,
        [SMEM] * 2 + [VMEM] * (len(args) - 2),
        scratch=[] if dtype == F32 else [pltpu.VMEM((n // 2 * len(chunks), width), F32)],
        flops=2 * n * n * width * len(chunks),
        nbytes=10 * n * width,
        name="forward",
        after=after,
    )


def backward_kernel(
    n_seq, kind, chunks, later, earlier, halves, given, place_ref, ids_ref, row_ref, col_ref, q_ref, k_ref, kt_ref, v_ref, *refs
):
    refs = list(refs)
    g_refs = [refs.pop(0) for _ in range(max(halves, 1))]
    add_q_ref, add_k_ref, slope_q_ref, slope_k_ref = [refs.pop(0) if x else None for x in given]
    gq_ref, gk_ref = refs.pop(0), refs.pop(0)
    sum_q_ref = gq_ref if slope_q_ref is None else refs.pop(0)
    sum_k_ref = gk_ref if slope_k_ref is None else refs.pop(0)
    n, width = q_ref.shape
    g_ref = g_refs[0]
    if halves == 2:
        g_ref = refs.pop(0)
        g_ref[: n // 2, :] = g_refs[0][...]
        g_ref[n // 2 :, :] = g_refs[1][...]
    me = place_ref[1]
    added = 0 if add_q_ref is None else add_q_ref.shape[0]
    if added:
        sum_q_ref[:added, :] = add_q_ref[...]
    if added < sum_q_ref.shape[0]:
        sum_q_ref[added:, :] = jnp.zeros_like(sum_q_ref[added:, :])
    if kind != "own":
        sum_k_ref[...] = jnp.zeros_like(sum_k_ref) if add_k_ref is None else add_k_ref[...]

    def part(rows, keys, offset, first):
        mask = ids_of(col_ref, me - earlier, keys, n, n_seq, 0) == ids_of(row_ref, me + later, rows, n, n_seq, 1)
        if offset is not None:
            mask &= lax.broadcasted_iota(jnp.int32, mask.shape, 0) <= offset + lax.broadcasted_iota(
                jnp.int32, mask.shape, 1
            )
        for h in range(HEADS):
            cols = slice(h * HD, (h + 1) * HD)
            k_cols = slice(width + h * HD, width + (h + 1) * HD)
            g = g_ref[rows, cols]
            half = dot_nt(k_ref[keys, cols], q_ref[rows, cols]) * HALF_SCALE
            bend = jnp.where(mask, 1.0 + jnp.tanh(half), 0.0)
            value = half * bend
            weights = value.astype(BF16)
            grads = (dot_nt(v_ref[keys, cols], g) * (bend + value * (2.0 - bend))).astype(BF16)
            part_v = dot(weights, g)
            part_k = dot(grads, q_ref[rows, cols]) * HALF_SCALE
            part_q = dot(kt_ref[cols, keys], grads).T * HALF_SCALE
            sum_k_ref[keys, cols] = part_v if first else sum_k_ref[keys, cols] + part_v
            sum_k_ref[keys, k_cols] = part_k if first else sum_k_ref[keys, k_cols] + part_k
            sum_q_ref[rows, cols] += part_q

    pair_loop(kind, chunks, later, earlier, place_ref, ids_ref, n, n_seq, part)
    if slope_q_ref is not None:
        gq_ref[...] = (sum_q_ref[...] * slope_q_ref[...].astype(F32)).astype(BF16)
    if slope_k_ref is not None:
        gk_ref[...] = (sum_k_ref[...] * slope_k_ref[...].astype(F32)).astype(BF16)


def backward(
    users, kind, q, keys, v, grads, later=0, earlier=0, add_q=None, add_k=None, slope_q=None, slope_k=None,
    chunks=(0, 1), after=()
):
    n, width = q.shape
    halves = len(grads) if isinstance(grads, list) else 0
    optional = [add_q, add_k, slope_q, slope_k]
    given = [x is not None for x in optional]
    args = [*users, q, *keys, v, *(grads if halves else [grads])] + [x for x in optional if x is not None]
    q_rows = n if 1 in chunks else n // 2
    scratch = [] if slope_q is None else [pltpu.VMEM((q_rows, width), F32)]
    scratch += [] if slope_k is None else [pltpu.VMEM((n, 2 * width), F32)]
    scratch += [pltpu.VMEM((n, width), BF16)] if halves == 2 else []
    return call(
        functools.partial(
            backward_kernel, lax.axis_size("seq"), kind, chunks, later, earlier, halves, given
        ),
        [
            like(q_rows, width, F32 if slope_q is None else BF16),
            like(n, 2 * width, F32 if slope_k is None else BF16),
        ],
        args,
        [SMEM] * 2 + [VMEM] * (len(args) - 2),
        scratch=scratch,
        flops=5 * n * n * width * len(chunks),
        nbytes=20 * n * width,
        name="backward",
        after=after,
    )


def gate_kernel(start, far, *refs):
    refs = list(refs)
    far_refs = [refs.pop(0) for _ in range(far)]
    own_ref, gg_ref, u_ref, slope_ref = refs[:4]
    outs = refs[-3:] if start == 0 else refs[-4:-1]
    n = far_refs[0].shape[0] if far_refs else own_ref.shape[0]
    rows = slice(start, start + n)
    attended = own_ref[rows, :]
    for far_ref in far_refs:
        attended = attended + far_ref[...].astype(F32)
    normed, inverse = centred(attended)
    gate = u_ref[rows, :].astype(F32)
    grad = gg_ref[rows, :]
    width = u_ref.shape[1]
    grad_attended = back(normed, inverse, grad * gate).astype(BF16)
    results = [
        grad_attended,
        (normed * gate).astype(BF16),
        (grad * normed * slope_ref[rows, :width].astype(F32)).astype(BF16),
    ]
    for out, result in zip(outs, results):
        out[rows, :] = result
    if start:
        refs[-1][...] = grad_attended
        for out, before in zip(outs, refs[4:7]):
            out[:start, :] = before[...]


def product_kernel(x_ref, w_ref, out_ref):
    out_ref[...] = dot_nt(x_ref[...], w_ref[...]).astype(out_ref.dtype)


def output_kernel(gated_ref, w_ref, tokens_ref, out_ref, flag_ref):
    flag_ref[...] = jnp.zeros_like(flag_ref)
    out_ref[...] = (dot(gated_ref[...], w_ref[...]) + tokens_ref[...].astype(F32)).astype(BF16)


def far_kernel(x_ref, wv_ref, wk_ref, out_ref):
    width = wv_ref.shape[1]
    out_ref[...] = (
        dot_nt(x_ref[:, :width], wv_ref[...]) + dot_nt(x_ref[:, width:], wk_ref[...])
    ).astype(out_ref.dtype)


def near_kernel(gu_ref, gvk_ref, gq_ref, wu_ref, wv_ref, wq_ref, wk_ref, out_ref):
    width = wv_ref.shape[1]
    out_ref[...] = (
        dot_nt(gu_ref[...], wu_ref[...])
        + dot_nt(gvk_ref[:, :width], wv_ref[...])
        + dot_nt(gq_ref[...], wq_ref[...])
        + dot_nt(gvk_ref[:, width:], wk_ref[...])
    )


def mid_kernel(count, near_ref, tokens_ref, cotangent_ref, *refs):
    far_refs, refs = refs[:count], refs[count:]
    if count:
        w_ref, sum_ref, scaled_ref, inverse_ref, held_ref, sem = refs
        width = held_ref.shape[1]
        fetch = pltpu.make_async_copy(w_ref.at[:, 2 * width : 3 * width], held_ref, sem)
        fetch.start()
    else:
        sum_ref, scaled_ref, inverse_ref = refs
    scaled, inverse = centred(tokens_ref[...].astype(F32))
    scaled_ref[...] = scaled.astype(BF16)
    inverse_ref[...] = jnp.broadcast_to(inverse, inverse_ref.shape)
    grad = near_ref[...]
    if count:
        fetch.wait()
        for gq_ref in far_refs:
            grad = grad + dot_nt(gq_ref[...], held_ref[...])
    sum_ref[...] = back(scaled, inverse, grad) + cotangent_ref[...].astype(F32)


def tokens_kernel(count, sum_ref, scaled_ref, inverse_ref, *refs):
    far_refs, (out_ref, flag_ref, far, out, far_sem, out_sem) = refs[:count], refs[count:]
    flag_ref[...] = jnp.zeros_like(flag_ref)
    chunks = far_sem.shape[1]
    step = out.shape[0] // chunks

    def rows(c):
        return pl.ds(c * step, step)

    fetches = [
        [pltpu.make_async_copy(ref.at[rows(c)], far.at[i, rows(c)], far_sem.at[i, c]) for i, ref in enumerate(far_refs)]
        for c in range(chunks)
    ]
    puts = [pltpu.make_async_copy(out.at[rows(c)], out_ref.at[rows(c)], out_sem.at[c]) for c in range(chunks)]
    for fetch in fetches:
        for copy in fetch:
            copy.start()
    for c in range(chunks):
        for copy in fetches[c]:
            copy.wait()
        grad = far[0, rows(c)].astype(F32)
        for i in range(1, count):
            grad = grad + far[i, rows(c)].astype(F32)
        part = back(scaled_ref[rows(c), :].astype(F32), inverse_ref[rows(c), :1], grad)
        out[rows(c)] = (sum_ref[rows(c), :] + part).astype(BF16)
        puts[c].start()
    for put in puts:
        put.wait()


def orders(dp):
    bits = dp.bit_length() - 1
    return [0] + list(range(1, bits)), [0] + list(range(bits - 1, 0, -1))


def block_of(me, slot, dp):
    bits = dp.bit_length() - 1
    clear, set_ = [
        sum(((slot >> (bits - 1 - p)) & 1) << order[p] for p in range(bits)) for order in orders(dp)
    ]
    return me ^ jnp.where((me & 1) == (slot >> (bits - 1)), clear, set_)


def weight_kernel(dp, half, parts, place_ref, *refs):
    out_ref = refs[-1]
    n_slots, rows = out_ref.shape[0], out_ref.shape[1]
    blocks = [block_of(place_ref[0], s, dp) for s in range(half * n_slots, (half + 1) * n_slots)]
    taken, at = 0, 0
    for count, width in parts:
        total = None
        for _ in range(count):
            x_ref, g_ref = refs[taken], refs[taken + 1]
            taken += 2
            x = jnp.concatenate(
                [x_ref[:, pl.ds(pl.multiple_of(b * rows, rows), rows)] for b in blocks], axis=1
            )
            term = dot_tn(x, g_ref[...])
            total = term if total is None else total + term
        out_ref[:, :, at : at + width] = total.astype(BF16).reshape(n_slots, rows, width)
        at += width


def weight_half(place, parts, half, after=(), weight=8):
    dp = lax.axis_size("dp")
    d = parts[0][0][0].shape[1]
    rows = d // dp
    widths = [pairs[0][1].shape[1] for pairs in parts]
    if rows % 128:
        total = jnp.concatenate(
            [sum(dot_tn(x, g) for x, g in pairs).astype(BF16) for pairs in parts], axis=1
        )
        return jnp.stack(
            [
                lax.dynamic_slice_in_dim(total, block_of(place[0], s, dp) * rows, rows)
                for s in range(half * dp // 2, (half + 1) * dp // 2)
            ]
        )
    args = [a for pairs in parts for pair in pairs for a in pair]
    n = args[0].shape[0]
    return call(
        functools.partial(weight_kernel, dp, half, [(len(p), w) for p, w in zip(parts, widths)]),
        jax.ShapeDtypeStruct((dp // 2, rows, sum(widths)), BF16),
        [place] + args,
        [SMEM] + [VMEM] * len(args),
        flops=sum(n * d * w * len(p) for p, w in zip(parts, widths)),
        nbytes=d * sum(widths),
        name="weights",
        after=after,
        weight=weight,
    )


def halve_kernel(mine_ref, other_ref, send_ref, keep_ref):
    half = send_ref.shape[0]
    total = mine_ref[...].astype(F32) + other_ref[...].astype(F32)
    send_ref[...] = total[half:].astype(BF16)
    keep_ref[...] = total[:half].astype(BF16)


def halve(mine, other, after=()):
    half = jax.ShapeDtypeStruct((mine.shape[0] // 2, *mine.shape[1:]), BF16)
    return call(halve_kernel, [half, half], [mine, other], name="halve", after=after)


def swap_dp(value, phase):
    dp = lax.axis_size("dp")
    pairs = [(i, i ^ (1 << orders(dp)[i & 1][phase])) for i in range(dp)]
    return lax.ppermute(value, "dp", pairs)


def first_share_kernel(count, place_ref, mine_ref, other_ref, keep_ref, send_ref, sum_ref):
    rows = sum_ref.shape[0] // count
    sum_ref[...] = mine_ref[0].astype(F32) + other_ref[0].astype(F32)

    def block(r):
        return sum_ref[pl.ds(pl.multiple_of((place_ref[1] ^ r) * rows, rows), rows), :]

    keep_ref[...] = jnp.concatenate([block(r) for r in range(0, count, 2)], axis=0)
    send_ref[...] = jnp.concatenate([block(r) for r in range(1, count, 2)], axis=0).astype(BF16)


def next_share_kernel(count, mine_ref, other_ref, keep_ref, send_ref):
    rows = mine_ref.shape[0] // count
    total = mine_ref[...] + other_ref[...].astype(F32)
    blocks = [total[r * rows : (r + 1) * rows] for r in range(count)]
    keep_ref[...] = jnp.concatenate(blocks[::2], axis=0)
    send_ref[...] = jnp.concatenate(blocks[1::2], axis=0).astype(BF16)


def swap_seq(value, bit):
    return lax.ppermute(value, "seq", [(i, i ^ bit) for i in range(lax.axis_size("seq"))])


def first_share(place, mine, other, after=()):
    rows, width = mine.shape[1], mine.shape[2]
    keep, send = call(
        functools.partial(first_share_kernel, lax.axis_size("seq")),
        [like(rows // 2, width, F32), like(rows // 2, width, BF16)],
        [place, mine, other],
        [SMEM, VMEM, VMEM],
        scratch=[pltpu.VMEM((rows, width), F32)],
        name="share",
        after=after,
    )
    return keep, swap_seq(send, 1)


def next_share(count, mine, other, after=()):
    rows, width = mine.shape
    keep, send = call(
        functools.partial(next_share_kernel, count),
        [like(rows // 2, width, F32), like(rows // 2, width, BF16)],
        [mine, other],
        name="share",
        after=after,
    )
    return keep, swap_seq(send, lax.axis_size("seq") // count)


def total_kernel(*refs):
    in_ref, out_ref = refs[-2:]
    count = (len(refs) - 2) // 2
    early, late = [
        sum([ref[...].astype(F32) for ref in part[1:]], part[0][...])
        for part in (refs[:count], refs[count : 2 * count])
    ]
    width = in_ref.shape[1] // 4
    in_ref[:, :width] = early[:, width:]
    in_ref[:, width : 2 * width] = late[:, :width]
    in_ref[:, 2 * width : 3 * width] = late[:, 2 * width :]
    in_ref[:, 3 * width :] = late[:, width : 2 * width]
    out_ref[...] = early[:, :width]


def local(tokens_in, user_ids, w_in, w_out, cotangent):
    tokens, id_table, upstream = tokens_in[0], user_ids[0], cotangent[0]
    n, d = tokens.shape
    width = w_out.shape[0]
    n_seq = lax.axis_size("seq")
    span = n_seq // 2
    up = (span + 1) // 2
    down = span - up
    place = jnp.stack([lax.axis_index("dp"), lax.axis_index("seq")]).astype(jnp.int32)
    ids = id_table.reshape(1, -1)
    users = [place, ids, ids, id_table.reshape(-1, 1)]

    far_tokens = [shift(tokens, by) for by in range(1, up + 1)]
    normed, slope_q, query, *sent = project(tokens, w_in, [2], "send" if down else True)
    if down:
        next_normed, next_query = [shift(x, -up) for x in sent]
    slope_u, gate, *_ = project(normed, w_in, [0], False)
    slope_vk, values, keys = project(normed, w_in, [1, 3], False, after=[gate])
    grad_gated = call(
        product_kernel, like(n, width, F32), [upstream, w_out], flops=2 * n * d * width,
        name="gated", after=[keys],
    )
    attended, keys_t = forward(users, "own", query, keys, values, after=[grad_gated])

    pieces = []
    for by in range(1, up + 1):
        pieces.append(project(far_tokens[by - 1], w_in, [1, 3], True, after=[attended]))
    far_attended = []
    order = [attended]
    if down:
        for half in (0, 1):
            partial = None
            for by in range(1, down + 1):
                _, _, far_values, far_keys = pieces[by - 1]
                [partial] = forward(
                    users, "far", next_query, far_keys, far_values, up, by, partial,
                    BF16 if by == down else F32, (half,), order,
                )
            order = [partial]
            far_attended.append(shift(partial, up))
    for by, (far_normed, slope, far_values, far_keys) in enumerate(pieces, 1):
        attended, far_t = forward(
            users, "near", query, far_keys, far_values, 0, by, attended, after=order
        )
        pieces[by - 1] = (far_normed, slope, far_values, (far_keys, far_t))

    gate_args = [attended, grad_gated, gate, slope_u]
    far_sums = [None] * up
    if down:
        first = call(
            functools.partial(gate_kernel, 0, 1),
            [like(n // 2, width, BF16)] * 3,
            [far_attended[0], *gate_args],
            flops=500 * n * width,
            name="gate",
        )
        next_grad = [shift(first[0], -up)]
        grad_q = None
        for by, (_, _, far_values, far_keys) in enumerate(pieces, 1):
            grad_q, far_sums[by - 1] = backward(
                users, "near", query, far_keys, far_values, [first[0]], 0, by, add_q=grad_q, chunks=(0,)
            )
        grad_attended, gated, grad_u, second = call(
            functools.partial(gate_kernel, n // 2, 1),
            [like(n, width, BF16)] * 3 + [like(n // 2, width, BF16)],
            [far_attended[1], *gate_args, *first],
            flops=500 * n * width,
            name="gate",
            after=[grad_q],
        )
        next_grad.append(shift(second, -up))
        rest = (1,)
    else:
        grad_attended, gated, grad_u = call(
            functools.partial(gate_kernel, 0, 0), [like(n, width, BF16)] * 3, gate_args, name="gate"
        )
        grad_q, rest = None, (0, 1)
    grad_q, grad_vk = backward(
        users, "own", query, (keys, keys_t), values, grad_attended, add_q=grad_q, slope_k=slope_vk,
        after=[next_normed] if down else [],
    )
    for by, (_, slope, far_values, far_keys) in enumerate(pieces, 1):
        grad_q, far_sums[by - 1] = backward(
            users, "near", query, far_keys, far_values, grad_attended, 0, by, add_q=grad_q,
            add_k=far_sums[by - 1], slope_q=slope_q if by == up else None,
            slope_k=None if by <= down else slope, chunks=rest,
        )
    if down:
        next_slope, _ = project(next_normed, w_in, [2], False, after=[grad_q])
    next_q = None
    for by in range(1, down + 1):
        _, slope, far_values, far_keys = pieces[by - 1]
        next_q, far_sums[by - 1] = backward(
            users, "far", next_query, far_keys, far_values, next_grad, up, by,
            add_q=next_q, add_k=far_sums[by - 1],
            slope_q=next_slope if by == down else None, slope_k=slope,
        )
    vk_pairs = [(normed, grad_vk)] + [(p[0], g) for p, g in zip(pieces, far_sums)]
    q_pairs = [(normed, grad_q)] + ([(next_normed, next_q)] if down else [])
    late = [vk_pairs, q_pairs]
    phases = range(2, lax.axis_size("dp").bit_length() - 1)
    order = [next_q] if down else [grad_q]
    late_send = weight_half(place, late, 1, weight=1)
    late_other = swap_dp(late_send, 0)
    late_mine = weight_half(place, late, 0, after=[late_send], weight=1)
    late_send, late_mine = halve(late_mine, late_other)
    late_other = swap_dp(late_send, 1)
    far_parts = []
    for by, grad in enumerate(far_sums, 1):
        part = call(
            far_kernel,
            like(n, d, BF16),
            [grad, w_in, w_in],
            [VMEM, columns(d, width, 1), columns(d, width, 3)],
            flops=4 * n * d * width,
            name="far", weight=1,
            after=[late_send],
        )
        far_parts.append(part)
    order = far_parts
    far_parts = [shift(part, -by) for by, part in enumerate(far_parts, 1)]
    next_q = [shift(next_q, up)] if down else []
    early = [[(upstream, gated)], [(normed, grad_u)]]
    early_send = weight_half(place, early, 1, after=order, weight=1)
    early_other = swap_dp(early_send, 0)
    early_mine = weight_half(place, early, 0, after=[early_send], weight=1)
    early_send, early_mine = halve(early_mine, early_other)
    early_other = swap_dp(early_send, 1)
    order = [early_send]
    near = call(
        near_kernel,
        like(n, d, F32),
        [grad_u, grad_vk, grad_q] + [w_in] * 4,
        [VMEM] * 3 + [columns(d, width, b) for b in range(4)],
        flops=8 * n * d * width,
        name="near", weight=1,
        after=order,
    )
    output, written = call(
        output_kernel, [like(n, d, BF16), like(8, 128, F32)], [gated, w_out, tokens], flops=2 * n * d * width,
        name="output", weight=1, after=[near],
    )
    order = [written]
    for phase in phases:
        late_send, late_mine = halve(late_mine, late_other, after=order)
        late_other = swap_dp(late_send, phase)
        early_send, early_mine = halve(early_mine, early_other, after=[late_send])
        early_other = swap_dp(early_send, phase)
        order = [early_send]
    late_sum = first_share(place, late_mine, late_other, order)
    early_sum = first_share(place, early_mine, early_other, late_sum[:1])
    mid, scaled, inverse = call(
        functools.partial(mid_kernel, len(next_q)),
        [like(n, d, F32), like(n, d, BF16), like(n, 128, F32)],
        [near, tokens, upstream, *next_q] + [w_in] * bool(next_q),
        [VMEM] * (3 + len(next_q)) + [pl.BlockSpec(memory_space=pl.ANY)] * bool(next_q),
        scratch=[pltpu.VMEM((d, width), BF16), pltpu.SemaphoreType.DMA] if next_q else [],
        name="mid", weight=0,
        after=early_sum[:1],
    )
    count = len(far_parts)
    grad_tokens, written = call(
        functools.partial(tokens_kernel, count),
        [like(n, d, BF16), like(8, 128, F32)],
        [mid, scaled, inverse, *far_parts],
        [VMEM] * 3 + [pl.BlockSpec(memory_space=pl.ANY)] * count,
        scratch=[
            pltpu.VMEM((count, n, d), BF16), pltpu.VMEM((n, d), BF16),
            pltpu.SemaphoreType.DMA((count, 4)), pltpu.SemaphoreType.DMA((4,)),
        ],
        name="tokens", weight=0,
        after=early_sum[:1],
        out_specs=[pl.BlockSpec(memory_space=pl.ANY), VMEM],
    )
    count = n_seq // 2
    while count > 1:
        early_sum = next_share(count, *early_sum, after=[written, late_sum[0]])
        late_sum = next_share(count, *late_sum, after=early_sum[:1])
        count //= 2
    rows = early_sum[0].shape[0]
    total_in, out_w = call(
        total_kernel,
        [like(rows, 4 * width, F32), like(rows, width, F32)],
        [*early_sum, *late_sum],
        name="total",
        after=[written],
    )
    return (output[None], grad_tokens[None], total_in, out_w.T)


def solution(mesh):
    in_specs = (P("dp", "seq", None), P("dp", None), P(), P(), P("dp", "seq", None))
    out_specs = (
        P("dp", "seq", None),
        P("dp", "seq", None),
        P(("dp", "seq"), None),
        P(None, ("dp", "seq")),
    )
    return jax.shard_map(local, mesh=mesh, in_specs=in_specs, out_specs=out_specs, check_vma=False)
```

```python
import functools
import math

import jax
import jax.numpy as jnp
from jax import lax
from jax.experimental import pallas as pl
from jax.experimental.pallas import tpu as pltpu
from jax.sharding import PartitionSpec as P

HEADS = 4
HD = 128
HALF_SCALE = 0.5 / math.sqrt(HD)
SCALE = 1.0 / math.sqrt(HD)
EPSILON = 1e-05
GRANT = 18 << 20
BF16 = jnp.bfloat16
F32 = jnp.float32
VMEM = pl.BlockSpec(memory_space=pltpu.VMEM)
SMEM = pl.BlockSpec(memory_space=pltpu.SMEM)


def shift(value, by):
    devices = lax.axis_size("seq")
    pairs = [(i, i + by) for i in range(devices) if 0 <= i + by < devices]
    return lax.ppermute(value, "seq", pairs)


def call(
    kernel, outs, args, specs=None, scratch=(), flops=0, nbytes=0, name=None, after=(), weight=8, out_specs=None
):
    first, last = len(args), len(args) + len(after)

    def body(*refs):
        kernel(*refs[:first], *refs[last:])

    return pl.pallas_call(
        body,
        grid=(1,),
        out_shape=outs,
        in_specs=(specs or [VMEM] * first) + [pl.BlockSpec(memory_space=pl.ANY)] * len(after),
        out_specs=out_specs or jax.tree.map(lambda _: VMEM, outs),
        scratch_shapes=scratch,
        compiler_params=pltpu.CompilerParams(vmem_limit_bytes=GRANT),
        cost_estimate=pl.CostEstimate(
            flops=weight * flops, bytes_accessed=nbytes, transcendentals=0
        ),
        name=name,
    )(*args, *after)


def columns(rows, width, block):
    return pl.BlockSpec((rows, width), lambda i: (0, block))


def like(rows, width, kind):
    return jax.ShapeDtypeStruct((rows, width), kind)


def dot(a, b):
    return jnp.dot(a, b, preferred_element_type=F32)


def dot_nt(a, b):
    return lax.dot_general(a, b, (((1,), (1,)), ((), ())), preferred_element_type=F32)


def dot_tn(a, b):
    return lax.dot_general(a, b, (((0,), (0,)), ((), ())), preferred_element_type=F32)


def centred(values):
    center = values - jnp.mean(values, axis=-1, keepdims=True)
    inverse = lax.rsqrt(jnp.mean(center * center, axis=-1, keepdims=True) + EPSILON)
    return center * inverse, inverse


def back(scaled, inverse, upstream):
    return inverse * (
        upstream
        - jnp.mean(upstream, axis=-1, keepdims=True)
        - scaled * jnp.mean(upstream * scaled, axis=-1, keepdims=True)
    )


def silu_and_slope(half):
    bend = 1.0 + jnp.tanh(half)
    value = half * bend
    return value, 0.5 * (bend + value * (2.0 - bend))


def project_kernel(raw, blocks, x_ref, *refs):
    w_refs, refs = refs[:blocks], refs[blocks:]
    if raw == "send":
        refs, (normed_send, act_send) = refs[:-2], refs[-2:]
    if raw:
        normed_ref, refs = refs[0], refs[1:]
        normed_ref[...] = centred(x_ref[...].astype(F32))[0].astype(BF16)
    else:
        normed_ref = x_ref
    slope_ref, act_refs = refs[0], refs[1:]
    width = slope_ref.shape[1] // blocks
    for b in range(blocks):
        value, slope = silu_and_slope(0.5 * dot(normed_ref[...], w_refs[b][...]))
        act_refs[b][...] = value.astype(BF16)
        slope_ref[:, b * width : (b + 1) * width] = slope.astype(BF16)
    if raw == "send":
        normed_send[...] = normed_ref[...]
        act_send[...] = act_refs[0][...]


def project(x, w_in, blocks, raw, after=()):
    n, d = x.shape
    width = w_in.shape[1] // 4
    outs = [like(n, d, BF16)] if raw else []
    outs += [like(n, width * len(blocks), BF16)] + [like(n, width, BF16)] * len(blocks)
    outs += [like(n, d, BF16), like(n, width, BF16)] if raw == "send" else []
    return call(
        functools.partial(project_kernel, raw, len(blocks)),
        outs,
        [x] + [w_in] * len(blocks),
        [VMEM] + [columns(d, width, b) for b in blocks],
        flops=2 * n * d * width * len(blocks),
        nbytes=2 * n * d + 2 * d * width * len(blocks),
        name="project",
        after=after,
    )


def pair_loop(kind, chunks, later, earlier, place_ref, ids_ref, n, n_seq, body):
    step = n // 2
    if kind == "own":
        for c in reversed(chunks):
            rows = c * step
            body(slice(rows, rows + step), slice(0, rows + step), rows, c == chunks[-1])
        return
    q_block, k_block = place_ref[1] + later, place_ref[1] - earlier
    valid = (q_block < n_seq) & (k_block >= 0)
    q_start, k_start = jnp.minimum(q_block, n_seq - 1) * n, jnp.maximum(k_block, 0) * n
    crosses = valid & (ids_ref[0, q_start + chunks[0] * step] == ids_ref[0, k_start + n - 1])
    if kind == "near":
        rows = slice(chunks[0] * step, (chunks[-1] + 1) * step)
        pl.when(crosses)(lambda: body(rows, slice(0, n), None, False))
        return

    @pl.loop(0, 2 * len(chunks))
    def _(i):
        row = pl.multiple_of((chunks[0] + i // 2) * step, step)
        key = pl.multiple_of((i % 2) * step, step)
        shared = ids_ref[0, q_start + row] == ids_ref[0, k_start + key + step - 1]
        pl.when(valid & shared)(
            lambda: body(pl.ds(row, step), pl.ds(key, step), None, False)
        )


def extent(part):
    if isinstance(part, slice):
        return part.start, part.stop - part.start
    return part.start, part.size


def ids_of(ref, block, rows, n, n_seq, axis):
    first, size = extent(rows)
    start = pl.multiple_of(jnp.clip(block, 0, n_seq - 1) * n, n) + first
    start = pl.multiple_of(start, size) if not isinstance(first, int) else start
    return ref[pl.ds(start, size), :] if axis == 0 else ref[:, pl.ds(start, size)]


def forward_kernel(
    n_seq, kind, chunks, later, earlier, more, place_ref, ids_ref, row_ref, col_ref, q_ref, k_ref, v_ref, *refs
):
    refs = list(refs)
    add_ref = refs.pop(0) if more else None
    out_ref = refs.pop(0)
    if kind != "far":
        refs.pop(0)[...] = k_ref[...].T
    sum_ref = refs.pop(0) if refs else out_ref
    n = q_ref.shape[0]
    base = chunks[0] * (n // 2)
    me = place_ref[1]
    if more or kind != "own":
        sum_ref[...] = add_ref[...] if more else jnp.zeros_like(sum_ref)

    def part(rows, keys, offset, first):
        first_row, size = extent(rows)
        out = slice(first_row - base, first_row - base + size) if kind != "far" else slice(0, size)
        mask = ids_of(col_ref, me + later, rows, n, n_seq, 0) == ids_of(row_ref, me - earlier, keys, n, n_seq, 1)
        if offset is not None:
            mask &= lax.broadcasted_iota(jnp.int32, mask.shape, 1) <= offset + lax.broadcasted_iota(
                jnp.int32, mask.shape, 0
            )
        for h in range(HEADS):
            cols = slice(h * HD, (h + 1) * HD)
            half = dot_nt(q_ref[rows, cols], k_ref[keys, cols]) * HALF_SCALE
            weights = jnp.where(mask, half * (1.0 + jnp.tanh(half)), 0.0).astype(BF16)
            term = dot(weights, v_ref[keys, cols])
            sum_ref[out, cols] = term if kind == "own" and not more else sum_ref[out, cols] + term

    pair_loop(kind, chunks, later, earlier, place_ref, ids_ref, n, n_seq, part)
    if sum_ref is not out_ref:
        out_ref[...] = sum_ref[...].astype(out_ref.dtype)


def forward(users, kind, q, k, v, later=0, earlier=0, add=None, dtype=F32, chunks=(0, 1), after=()):
    n, width = q.shape
    args = [*users, q, k, v] + ([] if add is None else [add])
    return call(
        functools.partial(
            forward_kernel, lax.axis_size("seq"), kind, chunks, later, earlier, add is not None
        ),
        [like(n // 2 * len(chunks), width, dtype)] + ([] if kind == "far" else [like(width, n, BF16)]),
        args,
        [SMEM] * 2 + [VMEM] * (len(args) - 2),
        scratch=[] if dtype == F32 else [pltpu.VMEM((n // 2 * len(chunks), width), F32)],
        flops=2 * n * n * width * len(chunks),
        nbytes=10 * n * width,
        name="forward",
        after=after,
    )


def backward_kernel(
    n_seq, kind, chunks, later, earlier, halves, given, place_ref, ids_ref, row_ref, col_ref, q_ref, k_ref, kt_ref, v_ref, *refs
):
    refs = list(refs)
    g_refs = [refs.pop(0) for _ in range(max(halves, 1))]
    add_q_ref, add_k_ref, slope_q_ref, slope_k_ref = [refs.pop(0) if x else None for x in given]
    gq_ref, gk_ref = refs.pop(0), refs.pop(0)
    sum_q_ref = gq_ref if slope_q_ref is None else refs.pop(0)
    sum_k_ref = gk_ref if slope_k_ref is None else refs.pop(0)
    n, width = q_ref.shape
    g_ref = g_refs[0]
    if halves == 2:
        g_ref = refs.pop(0)
        g_ref[: n // 2, :] = g_refs[0][...]
        g_ref[n // 2 :, :] = g_refs[1][...]
    me = place_ref[1]
    added = 0 if add_q_ref is None else add_q_ref.shape[0]
    if added:
        sum_q_ref[:added, :] = add_q_ref[...]
    if added < sum_q_ref.shape[0]:
        sum_q_ref[added:, :] = jnp.zeros_like(sum_q_ref[added:, :])
    if kind != "own":
        sum_k_ref[...] = jnp.zeros_like(sum_k_ref) if add_k_ref is None else add_k_ref[...]

    def part(rows, keys, offset, first):
        mask = ids_of(col_ref, me - earlier, keys, n, n_seq, 0) == ids_of(row_ref, me + later, rows, n, n_seq, 1)
        if offset is not None:
            mask &= lax.broadcasted_iota(jnp.int32, mask.shape, 0) <= offset + lax.broadcasted_iota(
                jnp.int32, mask.shape, 1
            )
        for h in range(HEADS):
            cols = slice(h * HD, (h + 1) * HD)
            k_cols = slice(width + h * HD, width + (h + 1) * HD)
            g = g_ref[rows, cols]
            half = dot_nt(k_ref[keys, cols], q_ref[rows, cols]) * HALF_SCALE
            bend = jnp.where(mask, 1.0 + jnp.tanh(half), 0.0)
            value = half * bend
            weights = value.astype(BF16)
            grads = (dot_nt(v_ref[keys, cols], g) * (bend + value * (2.0 - bend))).astype(BF16)
            part_v = dot(weights, g)
            part_k = dot(grads, q_ref[rows, cols]) * HALF_SCALE
            part_q = dot(kt_ref[cols, keys], grads).T * HALF_SCALE
            sum_k_ref[keys, cols] = part_v if first else sum_k_ref[keys, cols] + part_v
            sum_k_ref[keys, k_cols] = part_k if first else sum_k_ref[keys, k_cols] + part_k
            sum_q_ref[rows, cols] += part_q

    pair_loop(kind, chunks, later, earlier, place_ref, ids_ref, n, n_seq, part)
    if slope_q_ref is not None:
        gq_ref[...] = (sum_q_ref[...] * slope_q_ref[...].astype(F32)).astype(BF16)
    if slope_k_ref is not None:
        gk_ref[...] = (sum_k_ref[...] * slope_k_ref[...].astype(F32)).astype(BF16)


def backward(
    users, kind, q, keys, v, grads, later=0, earlier=0, add_q=None, add_k=None, slope_q=None, slope_k=None,
    chunks=(0, 1), after=()
):
    n, width = q.shape
    halves = len(grads) if isinstance(grads, list) else 0
    optional = [add_q, add_k, slope_q, slope_k]
    given = [x is not None for x in optional]
    args = [*users, q, *keys, v, *(grads if halves else [grads])] + [x for x in optional if x is not None]
    q_rows = n if 1 in chunks else n // 2
    scratch = [] if slope_q is None else [pltpu.VMEM((q_rows, width), F32)]
    scratch += [] if slope_k is None else [pltpu.VMEM((n, 2 * width), F32)]
    scratch += [pltpu.VMEM((n, width), BF16)] if halves == 2 else []
    return call(
        functools.partial(
            backward_kernel, lax.axis_size("seq"), kind, chunks, later, earlier, halves, given
        ),
        [
            like(q_rows, width, F32 if slope_q is None else BF16),
            like(n, 2 * width, F32 if slope_k is None else BF16),
        ],
        args,
        [SMEM] * 2 + [VMEM] * (len(args) - 2),
        scratch=scratch,
        flops=5 * n * n * width * len(chunks),
        nbytes=20 * n * width,
        name="backward",
        after=after,
    )


def gate_kernel(start, far, *refs):
    refs = list(refs)
    far_refs = [refs.pop(0) for _ in range(far)]
    own_ref, gg_ref, u_ref, slope_ref = refs[:4]
    outs = refs[-3:] if start == 0 else refs[-4:-1]
    n = far_refs[0].shape[0] if far_refs else own_ref.shape[0]
    rows = slice(start, start + n)
    attended = own_ref[rows, :]
    for far_ref in far_refs:
        attended = attended + far_ref[...].astype(F32)
    normed, inverse = centred(attended)
    gate = u_ref[rows, :].astype(F32)
    grad = gg_ref[rows, :]
    width = u_ref.shape[1]
    grad_attended = back(normed, inverse, grad * gate).astype(BF16)
    results = [
        grad_attended,
        (normed * gate).astype(BF16),
        (grad * normed * slope_ref[rows, :width].astype(F32)).astype(BF16),
    ]
    for out, result in zip(outs, results):
        out[rows, :] = result
    if start:
        refs[-1][...] = grad_attended
        for out, before in zip(outs, refs[4:7]):
            out[:start, :] = before[...]


def product_kernel(x_ref, w_ref, out_ref):
    out_ref[...] = dot_nt(x_ref[...], w_ref[...]).astype(out_ref.dtype)


def output_kernel(gated_ref, w_ref, tokens_ref, out_ref, flag_ref):
    flag_ref[...] = jnp.zeros_like(flag_ref)
    out_ref[...] = (dot(gated_ref[...], w_ref[...]) + tokens_ref[...].astype(F32)).astype(BF16)


def far_kernel(x_ref, wv_ref, wk_ref, out_ref):
    width = wv_ref.shape[1]
    out_ref[...] = (
        dot_nt(x_ref[:, :width], wv_ref[...]) + dot_nt(x_ref[:, width:], wk_ref[...])
    ).astype(out_ref.dtype)


def near_kernel(gu_ref, gvk_ref, gq_ref, wu_ref, wv_ref, wq_ref, wk_ref, out_ref):
    width = wv_ref.shape[1]
    out_ref[...] = (
        dot_nt(gu_ref[...], wu_ref[...])
        + dot_nt(gvk_ref[:, :width], wv_ref[...])
        + dot_nt(gq_ref[...], wq_ref[...])
        + dot_nt(gvk_ref[:, width:], wk_ref[...])
    )


def mid_kernel(count, near_ref, tokens_ref, cotangent_ref, *refs):
    far_refs, refs = refs[:count], refs[count:]
    if count:
        w_ref, sum_ref, scaled_ref, inverse_ref, held_ref, sem = refs
        width = held_ref.shape[1]
        fetch = pltpu.make_async_copy(w_ref.at[:, 2 * width : 3 * width], held_ref, sem)
        fetch.start()
    else:
        sum_ref, scaled_ref, inverse_ref = refs
    scaled, inverse = centred(tokens_ref[...].astype(F32))
    scaled_ref[...] = scaled.astype(BF16)
    inverse_ref[...] = jnp.broadcast_to(inverse, inverse_ref.shape)
    grad = near_ref[...]
    if count:
        fetch.wait()
        for gq_ref in far_refs:
            grad = grad + dot_nt(gq_ref[...], held_ref[...])
    sum_ref[...] = back(scaled, inverse, grad) + cotangent_ref[...].astype(F32)


def tokens_kernel(count, sum_ref, scaled_ref, inverse_ref, *refs):
    far_refs, (out_ref, flag_ref, far, out, far_sem, out_sem) = refs[:count], refs[count:]
    flag_ref[...] = jnp.zeros_like(flag_ref)
    chunks = far_sem.shape[1]
    step = out.shape[0] // chunks

    def rows(c):
        return pl.ds(c * step, step)

    fetches = [
        [pltpu.make_async_copy(ref.at[rows(c)], far.at[i, rows(c)], far_sem.at[i, c]) for i, ref in enumerate(far_refs)]
        for c in range(chunks)
    ]
    puts = [pltpu.make_async_copy(out.at[rows(c)], out_ref.at[rows(c)], out_sem.at[c]) for c in range(chunks)]
    for fetch in fetches:
        for copy in fetch:
            copy.start()
    for c in range(chunks):
        for copy in fetches[c]:
            copy.wait()
        grad = far[0, rows(c)].astype(F32)
        for i in range(1, count):
            grad = grad + far[i, rows(c)].astype(F32)
        part = back(scaled_ref[rows(c), :].astype(F32), inverse_ref[rows(c), :1], grad)
        out[rows(c)] = (sum_ref[rows(c), :] + part).astype(BF16)
        puts[c].start()
    for put in puts:
        put.wait()


def orders(dp):
    bits = dp.bit_length() - 1
    return [0] + list(range(1, bits)), [0] + list(range(bits - 1, 0, -1))


def block_of(me, slot, dp):
    bits = dp.bit_length() - 1
    clear, set_ = [
        sum(((slot >> (bits - 1 - p)) & 1) << order[p] for p in range(bits)) for order in orders(dp)
    ]
    return me ^ jnp.where((me & 1) == (slot >> (bits - 1)), clear, set_)


def weight_kernel(dp, half, parts, place_ref, *refs):
    out_ref = refs[-1]
    n_slots, rows = out_ref.shape[0], out_ref.shape[1]
    blocks = [block_of(place_ref[0], s, dp) for s in range(half * n_slots, (half + 1) * n_slots)]
    taken, at = 0, 0
    for count, width in parts:
        total = None
        for _ in range(count):
            x_ref, g_ref = refs[taken], refs[taken + 1]
            taken += 2
            x = jnp.concatenate(
                [x_ref[:, pl.ds(pl.multiple_of(b * rows, rows), rows)] for b in blocks], axis=1
            )
            term = dot_tn(x, g_ref[...])
            total = term if total is None else total + term
        out_ref[:, :, at : at + width] = total.astype(BF16).reshape(n_slots, rows, width)
        at += width


def weight_half(place, parts, half, after=(), weight=8):
    dp = lax.axis_size("dp")
    d = parts[0][0][0].shape[1]
    rows = d // dp
    widths = [pairs[0][1].shape[1] for pairs in parts]
    if rows % 128:
        total = jnp.concatenate(
            [sum(dot_tn(x, g) for x, g in pairs).astype(BF16) for pairs in parts], axis=1
        )
        return jnp.stack(
            [
                lax.dynamic_slice_in_dim(total, block_of(place[0], s, dp) * rows, rows)
                for s in range(half * dp // 2, (half + 1) * dp // 2)
            ]
        )
    args = [a for pairs in parts for pair in pairs for a in pair]
    n = args[0].shape[0]
    return call(
        functools.partial(weight_kernel, dp, half, [(len(p), w) for p, w in zip(parts, widths)]),
        jax.ShapeDtypeStruct((dp // 2, rows, sum(widths)), BF16),
        [place] + args,
        [SMEM] + [VMEM] * len(args),
        flops=sum(n * d * w * len(p) for p, w in zip(parts, widths)),
        nbytes=d * sum(widths),
        name="weights",
        after=after,
        weight=weight,
    )


def halve_kernel(mine_ref, other_ref, send_ref, keep_ref):
    half = send_ref.shape[0]
    total = mine_ref[...].astype(F32) + other_ref[...].astype(F32)
    send_ref[...] = total[half:].astype(BF16)
    keep_ref[...] = total[:half].astype(BF16)


def halve(mine, other, after=()):
    half = jax.ShapeDtypeStruct((mine.shape[0] // 2, *mine.shape[1:]), BF16)
    return call(halve_kernel, [half, half], [mine, other], name="halve", after=after)


def swap_dp(value, phase):
    dp = lax.axis_size("dp")
    pairs = [(i, i ^ (1 << orders(dp)[i & 1][phase])) for i in range(dp)]
    return lax.ppermute(value, "dp", pairs)


def first_share_kernel(count, place_ref, mine_ref, other_ref, keep_ref, send_ref, sum_ref):
    rows = sum_ref.shape[0] // count
    sum_ref[...] = mine_ref[0].astype(F32) + other_ref[0].astype(F32)

    def block(r):
        return sum_ref[pl.ds(pl.multiple_of((place_ref[1] ^ r) * rows, rows), rows), :]

    keep_ref[...] = jnp.concatenate([block(r) for r in range(0, count, 2)], axis=0)
    send_ref[...] = jnp.concatenate([block(r) for r in range(1, count, 2)], axis=0).astype(BF16)


def next_share_kernel(count, mine_ref, other_ref, keep_ref, send_ref):
    rows = mine_ref.shape[0] // count
    total = mine_ref[...] + other_ref[...].astype(F32)
    blocks = [total[r * rows : (r + 1) * rows] for r in range(count)]
    keep_ref[...] = jnp.concatenate(blocks[::2], axis=0)
    send_ref[...] = jnp.concatenate(blocks[1::2], axis=0).astype(BF16)


def swap_seq(value, bit):
    return lax.ppermute(value, "seq", [(i, i ^ bit) for i in range(lax.axis_size("seq"))])


def first_share(place, mine, other, after=()):
    rows, width = mine.shape[1], mine.shape[2]
    keep, send = call(
        functools.partial(first_share_kernel, lax.axis_size("seq")),
        [like(rows // 2, width, F32), like(rows // 2, width, BF16)],
        [place, mine, other],
        [SMEM, VMEM, VMEM],
        scratch=[pltpu.VMEM((rows, width), F32)],
        name="share",
        after=after,
    )
    return keep, swap_seq(send, 1)


def next_share(count, mine, other, after=()):
    rows, width = mine.shape
    keep, send = call(
        functools.partial(next_share_kernel, count),
        [like(rows // 2, width, F32), like(rows // 2, width, BF16)],
        [mine, other],
        name="share",
        after=after,
    )
    return keep, swap_seq(send, lax.axis_size("seq") // count)


def total_kernel(*refs):
    in_ref, out_ref = refs[-2:]
    count = (len(refs) - 2) // 2
    early, late = [
        sum([ref[...].astype(F32) for ref in part[1:]], part[0][...])
        for part in (refs[:count], refs[count : 2 * count])
    ]
    width = in_ref.shape[1] // 4
    in_ref[:, :width] = early[:, width:]
    in_ref[:, width : 2 * width] = late[:, :width]
    in_ref[:, 2 * width : 3 * width] = late[:, 2 * width :]
    in_ref[:, 3 * width :] = late[:, width : 2 * width]
    out_ref[...] = early[:, :width]


def local(tokens_in, user_ids, w_in, w_out, cotangent):
    tokens, id_table, upstream = tokens_in[0], user_ids[0], cotangent[0]
    n, d = tokens.shape
    width = w_out.shape[0]
    n_seq = lax.axis_size("seq")
    span = n_seq // 2
    up = (span + 1) // 2
    down = span - up
    place = jnp.stack([lax.axis_index("dp"), lax.axis_index("seq")]).astype(jnp.int32)
    ids = id_table.reshape(1, -1)
    users = [place, ids, ids, id_table.reshape(-1, 1)]

    far_tokens = [shift(tokens, by) for by in range(1, up + 1)]
    normed, slope_q, query, *sent = project(tokens, w_in, [2], "send" if down else True)
    if down:
        next_normed, next_query = [shift(x, -up) for x in sent]
    slope_u, gate, *_ = project(normed, w_in, [0], False)
    slope_vk, values, keys = project(normed, w_in, [1, 3], False, after=[gate])
    grad_gated = call(
        product_kernel, like(n, width, F32), [upstream, w_out], flops=2 * n * d * width,
        name="gated", after=[keys],
    )
    attended, keys_t = forward(users, "own", query, keys, values, after=[grad_gated])

    pieces = []
    for by in range(1, up + 1):
        pieces.append(project(far_tokens[by - 1], w_in, [1, 3], True, after=[attended]))
    far_attended = []
    order = [attended]
    if down:
        for half in (0, 1):
            partial = None
            for by in range(1, down + 1):
                _, _, far_values, far_keys = pieces[by - 1]
                [partial] = forward(
                    users, "far", next_query, far_keys, far_values, up, by, partial,
                    BF16 if by == down else F32, (half,), order,
                )
            order = [partial]
            far_attended.append(shift(partial, up))
    for by, (far_normed, slope, far_values, far_keys) in enumerate(pieces, 1):
        attended, far_t = forward(
            users, "near", query, far_keys, far_values, 0, by, attended, after=order
        )
        pieces[by - 1] = (far_normed, slope, far_values, (far_keys, far_t))

    gate_args = [attended, grad_gated, gate, slope_u]
    far_sums = [None] * up
    if down:
        first = call(
            functools.partial(gate_kernel, 0, 1),
            [like(n // 2, width, BF16)] * 3,
            [far_attended[0], *gate_args],
            flops=500 * n * width,
            name="gate",
        )
        next_grad = [shift(first[0], -up)]
        grad_q = None
        for by, (_, _, far_values, far_keys) in enumerate(pieces, 1):
            grad_q, far_sums[by - 1] = backward(
                users, "near", query, far_keys, far_values, [first[0]], 0, by, add_q=grad_q, chunks=(0,)
            )
        grad_attended, gated, grad_u, second = call(
            functools.partial(gate_kernel, n // 2, 1),
            [like(n, width, BF16)] * 3 + [like(n // 2, width, BF16)],
            [far_attended[1], *gate_args, *first],
            flops=500 * n * width,
            name="gate",
            after=[grad_q],
        )
        next_grad.append(shift(second, -up))
        rest = (1,)
    else:
        grad_attended, gated, grad_u = call(
            functools.partial(gate_kernel, 0, 0), [like(n, width, BF16)] * 3, gate_args, name="gate"
        )
        grad_q, rest = None, (0, 1)
    grad_q, grad_vk = backward(
        users, "own", query, (keys, keys_t), values, grad_attended, add_q=grad_q, slope_k=slope_vk,
        after=[next_normed] if down else [],
    )
    for by, (_, slope, far_values, far_keys) in enumerate(pieces, 1):
        grad_q, far_sums[by - 1] = backward(
            users, "near", query, far_keys, far_values, grad_attended, 0, by, add_q=grad_q,
            add_k=far_sums[by - 1], slope_q=slope_q if by == up else None,
            slope_k=None if by <= down else slope, chunks=rest,
        )
    if down:
        next_slope, _ = project(next_normed, w_in, [2], False, after=[grad_q])
    next_q = None
    for by in range(1, down + 1):
        _, slope, far_values, far_keys = pieces[by - 1]
        next_q, far_sums[by - 1] = backward(
            users, "far", next_query, far_keys, far_values, next_grad, up, by,
            add_q=next_q, add_k=far_sums[by - 1],
            slope_q=next_slope if by == down else None, slope_k=slope,
        )
    vk_pairs = [(normed, grad_vk)] + [(p[0], g) for p, g in zip(pieces, far_sums)]
    q_pairs = [(normed, grad_q)] + ([(next_normed, next_q)] if down else [])
    late = [vk_pairs, q_pairs]
    phases = range(2, lax.axis_size("dp").bit_length() - 1)
    order = [next_q] if down else [grad_q]
    late_send = weight_half(place, late, 1, weight=1)
    late_other = swap_dp(late_send, 0)
    far_parts = []
    for by, grad in enumerate(far_sums, 1):
        part = call(
            far_kernel,
            like(n, d, BF16),
            [grad, w_in, w_in],
            [VMEM, columns(d, width, 1), columns(d, width, 3)],
            flops=4 * n * d * width,
            name="far", weight=1,
            after=[late_send],
        )
        far_parts.append(part)
    late_mine = weight_half(place, late, 0, after=far_parts, weight=1)
    far_parts = [shift(part, -by) for by, part in enumerate(far_parts, 1)]
    late_send, late_mine = halve(late_mine, late_other)
    late_other = swap_dp(late_send, 1)
    order = [late_send]
    next_q = [shift(next_q, up)] if down else []
    early = [[(upstream, gated)], [(normed, grad_u)]]
    early_send = weight_half(place, early, 1, after=order, weight=1)
    early_other = swap_dp(early_send, 0)
    early_mine = weight_half(place, early, 0, after=[early_send], weight=1)
    early_send, early_mine = halve(early_mine, early_other)
    early_other = swap_dp(early_send, 1)
    order = [early_send]
    near = call(
        near_kernel,
        like(n, d, F32),
        [grad_u, grad_vk, grad_q] + [w_in] * 4,
        [VMEM] * 3 + [columns(d, width, b) for b in range(4)],
        flops=8 * n * d * width,
        name="near", weight=1,
        after=order,
    )
    output, written = call(
        output_kernel, [like(n, d, BF16), like(8, 128, F32)], [gated, w_out, tokens], flops=2 * n * d * width,
        name="output", weight=1, after=[near],
    )
    order = [written]
    for phase in phases:
        late_send, late_mine = halve(late_mine, late_other, after=order)
        late_other = swap_dp(late_send, phase)
        early_send, early_mine = halve(early_mine, early_other, after=[late_send])
        early_other = swap_dp(early_send, phase)
        order = [early_send]
    late_sum = first_share(place, late_mine, late_other, order)
    early_sum = first_share(place, early_mine, early_other, late_sum[:1])
    mid, scaled, inverse = call(
        functools.partial(mid_kernel, len(next_q)),
        [like(n, d, F32), like(n, d, BF16), like(n, 128, F32)],
        [near, tokens, upstream, *next_q] + [w_in] * bool(next_q),
        [VMEM] * (3 + len(next_q)) + [pl.BlockSpec(memory_space=pl.ANY)] * bool(next_q),
        scratch=[pltpu.VMEM((d, width), BF16), pltpu.SemaphoreType.DMA] if next_q else [],
        name="mid", weight=0,
        after=early_sum[:1],
    )
    count = len(far_parts)
    grad_tokens, written = call(
        functools.partial(tokens_kernel, count),
        [like(n, d, BF16), like(8, 128, F32)],
        [mid, scaled, inverse, *far_parts],
        [VMEM] * 3 + [pl.BlockSpec(memory_space=pl.ANY)] * count,
        scratch=[
            pltpu.VMEM((count, n, d), BF16), pltpu.VMEM((n, d), BF16),
            pltpu.SemaphoreType.DMA((count, 4)), pltpu.SemaphoreType.DMA((4,)),
        ],
        name="tokens", weight=0,
        after=early_sum[:1],
        out_specs=[pl.BlockSpec(memory_space=pl.ANY), VMEM],
    )
    count = n_seq // 2
    while count > 1:
        early_sum = next_share(count, *early_sum, after=[written, late_sum[0]])
        late_sum = next_share(count, *late_sum, after=early_sum[:1])
        count //= 2
    rows = early_sum[0].shape[0]
    total_in, out_w = call(
        total_kernel,
        [like(rows, 4 * width, F32), like(rows, width, F32)],
        [*early_sum, *late_sum],
        name="total",
        after=[written],
    )
    return (output[None], grad_tokens[None], total_in, out_w.T)


def solution(mesh):
    in_specs = (P("dp", "seq", None), P("dp", None), P(), P(), P("dp", "seq", None))
    out_specs = (
        P("dp", "seq", None),
        P("dp", "seq", None),
        P(("dp", "seq"), None),
        P(None, ("dp", "seq")),
    )
    return jax.shard_map(local, mesh=mesh, in_specs=in_specs, out_specs=out_specs, check_vma=False)
```

```python
import functools
import math

import jax
import jax.numpy as jnp
from jax import lax
from jax.experimental import pallas as pl
from jax.experimental.pallas import tpu as pltpu
from jax.sharding import PartitionSpec as P

HEADS = 4
HD = 128
HALF_SCALE = 0.5 / math.sqrt(HD)
SCALE = 1.0 / math.sqrt(HD)
EPSILON = 1e-05
GRANT = 18 << 20
BF16 = jnp.bfloat16
F32 = jnp.float32
VMEM = pl.BlockSpec(memory_space=pltpu.VMEM)
SMEM = pl.BlockSpec(memory_space=pltpu.SMEM)


def shift(value, by):
    devices = lax.axis_size("seq")
    pairs = [(i, i + by) for i in range(devices) if 0 <= i + by < devices]
    return lax.ppermute(value, "seq", pairs)


def call(
    kernel, outs, args, specs=None, scratch=(), flops=0, nbytes=0, name=None, after=(), weight=8, out_specs=None
):
    first, last = len(args), len(args) + len(after)

    def body(*refs):
        kernel(*refs[:first], *refs[last:])

    return pl.pallas_call(
        body,
        grid=(1,),
        out_shape=outs,
        in_specs=(specs or [VMEM] * first) + [pl.BlockSpec(memory_space=pl.ANY)] * len(after),
        out_specs=out_specs or jax.tree.map(lambda _: VMEM, outs),
        scratch_shapes=scratch,
        compiler_params=pltpu.CompilerParams(vmem_limit_bytes=GRANT),
        cost_estimate=pl.CostEstimate(
            flops=weight * flops, bytes_accessed=nbytes, transcendentals=0
        ),
        name=name,
    )(*args, *after)


def columns(rows, width, block):
    return pl.BlockSpec((rows, width), lambda i: (0, block))


def like(rows, width, kind):
    return jax.ShapeDtypeStruct((rows, width), kind)


def dot(a, b):
    return jnp.dot(a, b, preferred_element_type=F32)


def dot_nt(a, b):
    return lax.dot_general(a, b, (((1,), (1,)), ((), ())), preferred_element_type=F32)


def dot_tn(a, b):
    return lax.dot_general(a, b, (((0,), (0,)), ((), ())), preferred_element_type=F32)


def centred(values):
    center = values - jnp.mean(values, axis=-1, keepdims=True)
    inverse = lax.rsqrt(jnp.mean(center * center, axis=-1, keepdims=True) + EPSILON)
    return center * inverse, inverse


def back(scaled, inverse, upstream):
    return inverse * (
        upstream
        - jnp.mean(upstream, axis=-1, keepdims=True)
        - scaled * jnp.mean(upstream * scaled, axis=-1, keepdims=True)
    )


def silu_and_slope(half):
    bend = 1.0 + jnp.tanh(half)
    value = half * bend
    return value, 0.5 * (bend + value * (2.0 - bend))


def project_kernel(raw, blocks, x_ref, *refs):
    w_refs, refs = refs[:blocks], refs[blocks:]
    if raw == "send":
        refs, (normed_send, act_send) = refs[:-2], refs[-2:]
    if raw:
        normed_ref, refs = refs[0], refs[1:]
        normed_ref[...] = centred(x_ref[...].astype(F32))[0].astype(BF16)
    else:
        normed_ref = x_ref
    slope_ref, act_refs = refs[0], refs[1:]
    width = slope_ref.shape[1] // blocks
    for b in range(blocks):
        value, slope = silu_and_slope(0.5 * dot(normed_ref[...], w_refs[b][...]))
        act_refs[b][...] = value.astype(BF16)
        slope_ref[:, b * width : (b + 1) * width] = slope.astype(BF16)
    if raw == "send":
        normed_send[...] = normed_ref[...]
        act_send[...] = act_refs[0][...]


def project(x, w_in, blocks, raw, after=()):
    n, d = x.shape
    width = w_in.shape[1] // 4
    outs = [like(n, d, BF16)] if raw else []
    outs += [like(n, width * len(blocks), BF16)] + [like(n, width, BF16)] * len(blocks)
    outs += [like(n, d, BF16), like(n, width, BF16)] if raw == "send" else []
    return call(
        functools.partial(project_kernel, raw, len(blocks)),
        outs,
        [x] + [w_in] * len(blocks),
        [VMEM] + [columns(d, width, b) for b in blocks],
        flops=2 * n * d * width * len(blocks),
        nbytes=2 * n * d + 2 * d * width * len(blocks),
        name="project",
        after=after,
    )


def pair_loop(kind, chunks, later, earlier, place_ref, ids_ref, n, n_seq, body):
    step = n // 2
    if kind == "own":
        for c in reversed(chunks):
            rows = c * step
            body(slice(rows, rows + step), slice(0, rows + step), rows, c == chunks[-1])
        return
    q_block, k_block = place_ref[1] + later, place_ref[1] - earlier
    valid = (q_block < n_seq) & (k_block >= 0)
    q_start, k_start = jnp.minimum(q_block, n_seq - 1) * n, jnp.maximum(k_block, 0) * n
    crosses = valid & (ids_ref[0, q_start + chunks[0] * step] == ids_ref[0, k_start + n - 1])
    if kind == "near":
        rows = slice(chunks[0] * step, (chunks[-1] + 1) * step)
        pl.when(crosses)(lambda: body(rows, slice(0, n), None, False))
        return

    @pl.loop(0, 2 * len(chunks))
    def _(i):
        row = pl.multiple_of((chunks[0] + i // 2) * step, step)
        key = pl.multiple_of((i % 2) * step, step)
        shared = ids_ref[0, q_start + row] == ids_ref[0, k_start + key + step - 1]
        pl.when(valid & shared)(
            lambda: body(pl.ds(row, step), pl.ds(key, step), None, False)
        )


def extent(part):
    if isinstance(part, slice):
        return part.start, part.stop - part.start
    return part.start, part.size


def ids_of(ref, block, rows, n, n_seq, axis):
    first, size = extent(rows)
    start = pl.multiple_of(jnp.clip(block, 0, n_seq - 1) * n, n) + first
    start = pl.multiple_of(start, size) if not isinstance(first, int) else start
    return ref[pl.ds(start, size), :] if axis == 0 else ref[:, pl.ds(start, size)]


def forward_kernel(
    n_seq, kind, chunks, later, earlier, more, place_ref, ids_ref, row_ref, col_ref, q_ref, k_ref, v_ref, *refs
):
    refs = list(refs)
    add_ref = refs.pop(0) if more else None
    out_ref = refs.pop(0)
    if kind != "far":
        refs.pop(0)[...] = k_ref[...].T
    sum_ref = refs.pop(0) if refs else out_ref
    n = q_ref.shape[0]
    base = chunks[0] * (n // 2)
    me = place_ref[1]
    if more or kind != "own":
        sum_ref[...] = add_ref[...] if more else jnp.zeros_like(sum_ref)

    def part(rows, keys, offset, first):
        first_row, size = extent(rows)
        out = slice(first_row - base, first_row - base + size) if kind != "far" else slice(0, size)
        mask = ids_of(col_ref, me + later, rows, n, n_seq, 0) == ids_of(row_ref, me - earlier, keys, n, n_seq, 1)
        if offset is not None:
            mask &= lax.broadcasted_iota(jnp.int32, mask.shape, 1) <= offset + lax.broadcasted_iota(
                jnp.int32, mask.shape, 0
            )
        for h in range(HEADS):
            cols = slice(h * HD, (h + 1) * HD)
            half = dot_nt(q_ref[rows, cols], k_ref[keys, cols]) * HALF_SCALE
            weights = jnp.where(mask, half * (1.0 + jnp.tanh(half)), 0.0).astype(BF16)
            term = dot(weights, v_ref[keys, cols])
            sum_ref[out, cols] = term if kind == "own" and not more else sum_ref[out, cols] + term

    pair_loop(kind, chunks, later, earlier, place_ref, ids_ref, n, n_seq, part)
    if sum_ref is not out_ref:
        out_ref[...] = sum_ref[...].astype(out_ref.dtype)


def forward(users, kind, q, k, v, later=0, earlier=0, add=None, dtype=F32, chunks=(0, 1), after=()):
    n, width = q.shape
    args = [*users, q, k, v] + ([] if add is None else [add])
    return call(
        functools.partial(
            forward_kernel, lax.axis_size("seq"), kind, chunks, later, earlier, add is not None
        ),
        [like(n // 2 * len(chunks), width, dtype)] + ([] if kind == "far" else [like(width, n, BF16)]),
        args,
        [SMEM] * 2 + [VMEM] * (len(args) - 2),
        scratch=[] if dtype == F32 else [pltpu.VMEM((n // 2 * len(chunks), width), F32)],
        flops=2 * n * n * width * len(chunks),
        nbytes=10 * n * width,
        name="forward",
        after=after,
    )


def backward_kernel(
    n_seq, kind, chunks, later, earlier, halves, given, place_ref, ids_ref, row_ref, col_ref, q_ref, k_ref, kt_ref, v_ref, *refs
):
    refs = list(refs)
    g_refs = [refs.pop(0) for _ in range(max(halves, 1))]
    add_q_ref, add_k_ref, slope_q_ref, slope_k_ref = [refs.pop(0) if x else None for x in given]
    gq_ref, gk_ref = refs.pop(0), refs.pop(0)
    sum_q_ref = gq_ref if slope_q_ref is None else refs.pop(0)
    sum_k_ref = gk_ref if slope_k_ref is None else refs.pop(0)
    n, width = q_ref.shape
    g_ref = g_refs[0]
    if halves == 2:
        g_ref = refs.pop(0)
        g_ref[: n // 2, :] = g_refs[0][...]
        g_ref[n // 2 :, :] = g_refs[1][...]
    me = place_ref[1]
    added = 0 if add_q_ref is None else add_q_ref.shape[0]
    if added:
        sum_q_ref[:added, :] = add_q_ref[...]
    if added < sum_q_ref.shape[0]:
        sum_q_ref[added:, :] = jnp.zeros_like(sum_q_ref[added:, :])
    if kind != "own":
        sum_k_ref[...] = jnp.zeros_like(sum_k_ref) if add_k_ref is None else add_k_ref[...]

    def part(rows, keys, offset, first):
        mask = ids_of(col_ref, me - earlier, keys, n, n_seq, 0) == ids_of(row_ref, me + later, rows, n, n_seq, 1)
        if offset is not None:
            mask &= lax.broadcasted_iota(jnp.int32, mask.shape, 0) <= offset + lax.broadcasted_iota(
                jnp.int32, mask.shape, 1
            )
        for h in range(HEADS):
            cols = slice(h * HD, (h + 1) * HD)
            k_cols = slice(width + h * HD, width + (h + 1) * HD)
            g = g_ref[rows, cols]
            half = dot_nt(k_ref[keys, cols], q_ref[rows, cols]) * HALF_SCALE
            bend = jnp.where(mask, 1.0 + jnp.tanh(half), 0.0)
            value = half * bend
            weights = value.astype(BF16)
            grads = (dot_nt(v_ref[keys, cols], g) * (bend + value * (2.0 - bend))).astype(BF16)
            part_v = dot(weights, g)
            part_k = dot(grads, q_ref[rows, cols]) * HALF_SCALE
            part_q = dot(kt_ref[cols, keys], grads).T * HALF_SCALE
            sum_k_ref[keys, cols] = part_v if first else sum_k_ref[keys, cols] + part_v
            sum_k_ref[keys, k_cols] = part_k if first else sum_k_ref[keys, k_cols] + part_k
            sum_q_ref[rows, cols] += part_q

    pair_loop(kind, chunks, later, earlier, place_ref, ids_ref, n, n_seq, part)
    if slope_q_ref is not None:
        gq_ref[...] = (sum_q_ref[...] * slope_q_ref[...].astype(F32)).astype(BF16)
    if slope_k_ref is not None:
        gk_ref[...] = (sum_k_ref[...] * slope_k_ref[...].astype(F32)).astype(BF16)


def backward(
    users, kind, q, keys, v, grads, later=0, earlier=0, add_q=None, add_k=None, slope_q=None, slope_k=None,
    chunks=(0, 1), after=()
):
    n, width = q.shape
    halves = len(grads) if isinstance(grads, list) else 0
    optional = [add_q, add_k, slope_q, slope_k]
    given = [x is not None for x in optional]
    args = [*users, q, *keys, v, *(grads if halves else [grads])] + [x for x in optional if x is not None]
    q_rows = n if 1 in chunks else n // 2
    scratch = [] if slope_q is None else [pltpu.VMEM((q_rows, width), F32)]
    scratch += [] if slope_k is None else [pltpu.VMEM((n, 2 * width), F32)]
    scratch += [pltpu.VMEM((n, width), BF16)] if halves == 2 else []
    return call(
        functools.partial(
            backward_kernel, lax.axis_size("seq"), kind, chunks, later, earlier, halves, given
        ),
        [
            like(q_rows, width, F32 if slope_q is None else BF16),
            like(n, 2 * width, F32 if slope_k is None else BF16),
        ],
        args,
        [SMEM] * 2 + [VMEM] * (len(args) - 2),
        scratch=scratch,
        flops=5 * n * n * width * len(chunks),
        nbytes=20 * n * width,
        name="backward",
        after=after,
    )


def gate_kernel(start, far, *refs):
    refs = list(refs)
    far_refs = [refs.pop(0) for _ in range(far)]
    own_ref, gg_ref, u_ref, slope_ref = refs[:4]
    outs = refs[-3:] if start == 0 else refs[-4:-1]
    n = far_refs[0].shape[0] if far_refs else own_ref.shape[0]
    rows = slice(start, start + n)
    attended = own_ref[rows, :]
    for far_ref in far_refs:
        attended = attended + far_ref[...].astype(F32)
    normed, inverse = centred(attended)
    gate = u_ref[rows, :].astype(F32)
    grad = gg_ref[rows, :]
    width = u_ref.shape[1]
    grad_attended = back(normed, inverse, grad * gate).astype(BF16)
    results = [
        grad_attended,
        (normed * gate).astype(BF16),
        (grad * normed * slope_ref[rows, :width].astype(F32)).astype(BF16),
    ]
    for out, result in zip(outs, results):
        out[rows, :] = result
    if start:
        refs[-1][...] = grad_attended
        for out, before in zip(outs, refs[4:7]):
            out[:start, :] = before[...]


def product_kernel(x_ref, w_ref, out_ref):
    out_ref[...] = dot_nt(x_ref[...], w_ref[...]).astype(out_ref.dtype)


def output_kernel(gated_ref, w_ref, tokens_ref, out_ref, flag_ref):
    flag_ref[...] = jnp.zeros_like(flag_ref)
    out_ref[...] = (dot(gated_ref[...], w_ref[...]) + tokens_ref[...].astype(F32)).astype(BF16)


def far_kernel(x_ref, wv_ref, wk_ref, out_ref):
    width = wv_ref.shape[1]
    out_ref[...] = (
        dot_nt(x_ref[:, :width], wv_ref[...]) + dot_nt(x_ref[:, width:], wk_ref[...])
    ).astype(out_ref.dtype)


def near_kernel(gu_ref, gvk_ref, gq_ref, wu_ref, wv_ref, wq_ref, wk_ref, out_ref):
    width = wv_ref.shape[1]
    out_ref[...] = (
        dot_nt(gu_ref[...], wu_ref[...])
        + dot_nt(gvk_ref[:, :width], wv_ref[...])
        + dot_nt(gq_ref[...], wq_ref[...])
        + dot_nt(gvk_ref[:, width:], wk_ref[...])
    )


def mid_kernel(count, near_ref, tokens_ref, cotangent_ref, *refs):
    far_refs, refs = refs[:count], refs[count:]
    if count:
        w_ref, sum_ref, scaled_ref, inverse_ref, held_ref, sem = refs
        width = held_ref.shape[1]
        fetch = pltpu.make_async_copy(w_ref.at[:, 2 * width : 3 * width], held_ref, sem)
        fetch.start()
    else:
        sum_ref, scaled_ref, inverse_ref = refs
    scaled, inverse = centred(tokens_ref[...].astype(F32))
    scaled_ref[...] = scaled.astype(BF16)
    inverse_ref[...] = jnp.broadcast_to(inverse, inverse_ref.shape)
    grad = near_ref[...]
    if count:
        fetch.wait()
        for gq_ref in far_refs:
            grad = grad + dot_nt(gq_ref[...], held_ref[...])
    sum_ref[...] = back(scaled, inverse, grad) + cotangent_ref[...].astype(F32)


def tokens_kernel(count, sum_ref, scaled_ref, inverse_ref, *refs):
    far_refs, (out_ref, flag_ref, far, out, far_sem, out_sem) = refs[:count], refs[count:]
    flag_ref[...] = jnp.zeros_like(flag_ref)
    chunks = far_sem.shape[1]
    step = out.shape[0] // chunks

    def rows(c):
        return pl.ds(c * step, step)

    fetches = [
        [pltpu.make_async_copy(ref.at[rows(c)], far.at[i, rows(c)], far_sem.at[i, c]) for i, ref in enumerate(far_refs)]
        for c in range(chunks)
    ]
    puts = [pltpu.make_async_copy(out.at[rows(c)], out_ref.at[rows(c)], out_sem.at[c]) for c in range(chunks)]
    for fetch in fetches:
        for copy in fetch:
            copy.start()
    for c in range(chunks):
        for copy in fetches[c]:
            copy.wait()
        grad = far[0, rows(c)].astype(F32)
        for i in range(1, count):
            grad = grad + far[i, rows(c)].astype(F32)
        part = back(scaled_ref[rows(c), :].astype(F32), inverse_ref[rows(c), :1], grad)
        out[rows(c)] = (sum_ref[rows(c), :] + part).astype(BF16)
        puts[c].start()
    for put in puts:
        put.wait()


def orders(dp):
    bits = dp.bit_length() - 1
    return [0] + list(range(1, bits)), [0] + list(range(bits - 1, 0, -1))


def block_of(me, slot, dp):
    bits = dp.bit_length() - 1
    clear, set_ = [
        sum(((slot >> (bits - 1 - p)) & 1) << order[p] for p in range(bits)) for order in orders(dp)
    ]
    return me ^ jnp.where((me & 1) == (slot >> (bits - 1)), clear, set_)


def weight_kernel(dp, half, parts, place_ref, *refs):
    out_ref = refs[-1]
    n_slots, rows = out_ref.shape[0], out_ref.shape[1]
    blocks = [block_of(place_ref[0], s, dp) for s in range(half * n_slots, (half + 1) * n_slots)]
    taken, at = 0, 0
    for count, width in parts:
        total = None
        for _ in range(count):
            x_ref, g_ref = refs[taken], refs[taken + 1]
            taken += 2
            x = jnp.concatenate(
                [x_ref[:, pl.ds(pl.multiple_of(b * rows, rows), rows)] for b in blocks], axis=1
            )
            term = dot_tn(x, g_ref[...])
            total = term if total is None else total + term
        out_ref[:, :, at : at + width] = total.astype(BF16).reshape(n_slots, rows, width)
        at += width


def weight_half(place, parts, half, after=(), weight=8):
    dp = lax.axis_size("dp")
    d = parts[0][0][0].shape[1]
    rows = d // dp
    widths = [pairs[0][1].shape[1] for pairs in parts]
    if rows % 128:
        total = jnp.concatenate(
            [sum(dot_tn(x, g) for x, g in pairs).astype(BF16) for pairs in parts], axis=1
        )
        return jnp.stack(
            [
                lax.dynamic_slice_in_dim(total, block_of(place[0], s, dp) * rows, rows)
                for s in range(half * dp // 2, (half + 1) * dp // 2)
            ]
        )
    args = [a for pairs in parts for pair in pairs for a in pair]
    n = args[0].shape[0]
    return call(
        functools.partial(weight_kernel, dp, half, [(len(p), w) for p, w in zip(parts, widths)]),
        jax.ShapeDtypeStruct((dp // 2, rows, sum(widths)), BF16),
        [place] + args,
        [SMEM] + [VMEM] * len(args),
        flops=sum(n * d * w * len(p) for p, w in zip(parts, widths)),
        nbytes=d * sum(widths),
        name="weights",
        after=after,
        weight=weight,
    )


def halve_kernel(mine_ref, other_ref, send_ref, keep_ref):
    half = send_ref.shape[0]
    total = mine_ref[...].astype(F32) + other_ref[...].astype(F32)
    send_ref[...] = total[half:].astype(BF16)
    keep_ref[...] = total[:half].astype(BF16)


def halve(mine, other, after=()):
    half = jax.ShapeDtypeStruct((mine.shape[0] // 2, *mine.shape[1:]), BF16)
    return call(halve_kernel, [half, half], [mine, other], name="halve", after=after)


def swap_dp(value, phase):
    dp = lax.axis_size("dp")
    pairs = [(i, i ^ (1 << orders(dp)[i & 1][phase])) for i in range(dp)]
    return lax.ppermute(value, "dp", pairs)


def first_share_kernel(count, place_ref, mine_ref, other_ref, keep_ref, send_ref, sum_ref):
    rows = sum_ref.shape[0] // count
    sum_ref[...] = mine_ref[0].astype(F32) + other_ref[0].astype(F32)

    def block(r):
        return sum_ref[pl.ds(pl.multiple_of((place_ref[1] ^ r) * rows, rows), rows), :]

    keep_ref[...] = jnp.concatenate([block(r) for r in range(0, count, 2)], axis=0)
    send_ref[...] = jnp.concatenate([block(r) for r in range(1, count, 2)], axis=0).astype(BF16)


def next_share_kernel(count, mine_ref, other_ref, keep_ref, send_ref):
    rows = mine_ref.shape[0] // count
    total = mine_ref[...] + other_ref[...].astype(F32)
    blocks = [total[r * rows : (r + 1) * rows] for r in range(count)]
    keep_ref[...] = jnp.concatenate(blocks[::2], axis=0)
    send_ref[...] = jnp.concatenate(blocks[1::2], axis=0).astype(BF16)


def swap_seq(value, bit):
    return lax.ppermute(value, "seq", [(i, i ^ bit) for i in range(lax.axis_size("seq"))])


def first_share(place, mine, other, after=()):
    rows, width = mine.shape[1], mine.shape[2]
    keep, send = call(
        functools.partial(first_share_kernel, lax.axis_size("seq")),
        [like(rows // 2, width, F32), like(rows // 2, width, BF16)],
        [place, mine, other],
        [SMEM, VMEM, VMEM],
        scratch=[pltpu.VMEM((rows, width), F32)],
        name="share",
        after=after,
    )
    return keep, swap_seq(send, 1)


def next_share(count, mine, other, after=()):
    rows, width = mine.shape
    keep, send = call(
        functools.partial(next_share_kernel, count),
        [like(rows // 2, width, F32), like(rows // 2, width, BF16)],
        [mine, other],
        name="share",
        after=after,
    )
    return keep, swap_seq(send, lax.axis_size("seq") // count)


def total_kernel(*refs):
    in_ref, out_ref = refs[-2:]
    count = (len(refs) - 2) // 2
    early, late = [
        sum([ref[...].astype(F32) for ref in part[1:]], part[0][...])
        for part in (refs[:count], refs[count : 2 * count])
    ]
    width = in_ref.shape[1] // 4
    in_ref[:, :width] = early[:, width:]
    in_ref[:, width : 2 * width] = late[:, :width]
    in_ref[:, 2 * width : 3 * width] = late[:, 2 * width :]
    in_ref[:, 3 * width :] = late[:, width : 2 * width]
    out_ref[...] = early[:, :width]


def local(tokens_in, user_ids, w_in, w_out, cotangent):
    tokens, id_table, upstream = tokens_in[0], user_ids[0], cotangent[0]
    n, d = tokens.shape
    width = w_out.shape[0]
    n_seq = lax.axis_size("seq")
    span = n_seq // 2
    up = (span + 1) // 2
    down = span - up
    place = jnp.stack([lax.axis_index("dp"), lax.axis_index("seq")]).astype(jnp.int32)
    ids = id_table.reshape(1, -1)
    users = [place, ids, ids, id_table.reshape(-1, 1)]

    far_tokens = [shift(tokens, by) for by in range(1, up + 1)]
    normed, slope_q, query, *sent = project(tokens, w_in, [2], "send" if down else True)
    if down:
        next_normed, next_query = [shift(x, -up) for x in sent]
    slope_u, gate, *_ = project(normed, w_in, [0], False)
    slope_vk, values, keys = project(normed, w_in, [1, 3], False, after=[gate])
    grad_gated = call(
        product_kernel, like(n, width, F32), [upstream, w_out], flops=2 * n * d * width,
        name="gated", after=[keys],
    )
    attended, keys_t = forward(users, "own", query, keys, values, after=[grad_gated])

    pieces = []
    for by in range(1, up + 1):
        pieces.append(project(far_tokens[by - 1], w_in, [1, 3], True, after=[attended]))
    far_attended = []
    order = [attended]
    if down:
        for half in (0, 1):
            partial = None
            for by in range(1, down + 1):
                _, _, far_values, far_keys = pieces[by - 1]
                [partial] = forward(
                    users, "far", next_query, far_keys, far_values, up, by, partial,
                    BF16 if by == down else F32, (half,), order,
                )
            order = [partial]
            far_attended.append(shift(partial, up))
    for by, (far_normed, slope, far_values, far_keys) in enumerate(pieces, 1):
        attended, far_t = forward(
            users, "near", query, far_keys, far_values, 0, by, attended, after=order
        )
        pieces[by - 1] = (far_normed, slope, far_values, (far_keys, far_t))

    gate_args = [attended, grad_gated, gate, slope_u]
    far_sums = [None] * up
    if down:
        first = call(
            functools.partial(gate_kernel, 0, 1),
            [like(n // 2, width, BF16)] * 3,
            [far_attended[0], *gate_args],
            flops=500 * n * width,
            name="gate",
        )
        next_grad = [shift(first[0], -up)]
        grad_q = None
        for by, (_, _, far_values, far_keys) in enumerate(pieces, 1):
            grad_q, far_sums[by - 1] = backward(
                users, "near", query, far_keys, far_values, [first[0]], 0, by, add_q=grad_q, chunks=(0,)
            )
        grad_attended, gated, grad_u, second = call(
            functools.partial(gate_kernel, n // 2, 1),
            [like(n, width, BF16)] * 3 + [like(n // 2, width, BF16)],
            [far_attended[1], *gate_args, *first],
            flops=500 * n * width,
            name="gate",
            after=[grad_q],
        )
        next_grad.append(shift(second, -up))
        rest = (1,)
    else:
        grad_attended, gated, grad_u = call(
            functools.partial(gate_kernel, 0, 0), [like(n, width, BF16)] * 3, gate_args, name="gate"
        )
        grad_q, rest = None, (0, 1)
    grad_q, grad_vk = backward(
        users, "own", query, (keys, keys_t), values, grad_attended, add_q=grad_q, slope_k=slope_vk,
        after=[next_normed] if down else [],
    )
    for by, (_, slope, far_values, far_keys) in enumerate(pieces, 1):
        grad_q, far_sums[by - 1] = backward(
            users, "near", query, far_keys, far_values, grad_attended, 0, by, add_q=grad_q,
            add_k=far_sums[by - 1], slope_q=slope_q if by == up else None,
            slope_k=None if by <= down else slope, chunks=rest,
        )
    if down:
        next_slope, _ = project(next_normed, w_in, [2], False, after=[grad_q])
    next_q = None
    for by in range(1, down + 1):
        _, slope, far_values, far_keys = pieces[by - 1]
        next_q, far_sums[by - 1] = backward(
            users, "far", next_query, far_keys, far_values, next_grad, up, by,
            add_q=next_q, add_k=far_sums[by - 1],
            slope_q=next_slope if by == down else None, slope_k=slope,
        )
    vk_pairs = [(normed, grad_vk)] + [(p[0], g) for p, g in zip(pieces, far_sums)]
    q_pairs = [(normed, grad_q)] + ([(next_normed, next_q)] if down else [])
    late = [vk_pairs, q_pairs]
    phases = range(2, lax.axis_size("dp").bit_length() - 1)
    order = [next_q] if down else [grad_q]
    late_send = weight_half(place, late, 1, weight=1)
    late_other = swap_dp(late_send, 0)
    far_parts = []
    for by, grad in enumerate(far_sums, 1):
        part = call(
            far_kernel,
            like(n, d, BF16),
            [grad, w_in, w_in],
            [VMEM, columns(d, width, 1), columns(d, width, 3)],
            flops=4 * n * d * width,
            name="far", weight=1,
            after=[late_send],
        )
        far_parts.append(part)
    late_mine = weight_half(place, late, 0, after=far_parts, weight=1)
    far_parts = [shift(part, -by) for by, part in enumerate(far_parts, 1)]
    late_send, late_mine = halve(late_mine, late_other)
    late_other = swap_dp(late_send, 1)
    order = [late_send]
    next_q = [shift(next_q, up)] if down else []
    early = [[(upstream, gated)], [(normed, grad_u)]]
    early_send = weight_half(place, early, 1, after=order, weight=1)
    early_other = swap_dp(early_send, 0)
    early_mine = weight_half(place, early, 0, after=[early_send], weight=1)
    early_send, early_mine = halve(early_mine, early_other)
    early_other = swap_dp(early_send, 1)
    order = [early_send]
    near = call(
        near_kernel,
        like(n, d, F32),
        [grad_u, grad_vk, grad_q] + [w_in] * 4,
        [VMEM] * 3 + [columns(d, width, b) for b in range(4)],
        flops=8 * n * d * width,
        name="near", weight=1,
        after=order,
    )
    output, written = call(
        output_kernel, [like(n, d, BF16), like(8, 128, F32)], [gated, w_out, tokens], flops=2 * n * d * width,
        name="output", weight=1, after=[near],
    )
    order = [written]
    for phase in phases:
        late_send, late_mine = halve(late_mine, late_other, after=order)
        late_other = swap_dp(late_send, phase)
        early_send, early_mine = halve(
            early_mine, early_other, after=[late_send, *next_q]
        )
        early_other = swap_dp(early_send, phase)
        order = [early_send]
    late_sum = first_share(place, late_mine, late_other, order)
    early_sum = first_share(place, early_mine, early_other, late_sum[:1])
    mid, scaled, inverse = call(
        functools.partial(mid_kernel, len(next_q)),
        [like(n, d, F32), like(n, d, BF16), like(n, 128, F32)],
        [near, tokens, upstream, *next_q] + [w_in] * bool(next_q),
        [VMEM] * (3 + len(next_q)) + [pl.BlockSpec(memory_space=pl.ANY)] * bool(next_q),
        scratch=[pltpu.VMEM((d, width), BF16), pltpu.SemaphoreType.DMA] if next_q else [],
        name="mid", weight=0,
        after=early_sum[:1],
    )
    count = len(far_parts)
    grad_tokens, written = call(
        functools.partial(tokens_kernel, count),
        [like(n, d, BF16), like(8, 128, F32)],
        [mid, scaled, inverse, *far_parts],
        [VMEM] * 3 + [pl.BlockSpec(memory_space=pl.ANY)] * count,
        scratch=[
            pltpu.VMEM((count, n, d), BF16), pltpu.VMEM((n, d), BF16),
            pltpu.SemaphoreType.DMA((count, 4)), pltpu.SemaphoreType.DMA((4,)),
        ],
        name="tokens", weight=0,
        after=early_sum[:1],
        out_specs=[pl.BlockSpec(memory_space=pl.ANY), VMEM],
    )
    count = n_seq // 2
    while count > 1:
        early_sum = next_share(count, *early_sum, after=[written, late_sum[0]])
        late_sum = next_share(count, *late_sum, after=early_sum[:1])
        count //= 2
    rows = early_sum[0].shape[0]
    total_in, out_w = call(
        total_kernel,
        [like(rows, 4 * width, F32), like(rows, width, F32)],
        [*early_sum, *late_sum],
        name="total",
        after=[written],
    )
    return (output[None], grad_tokens[None], total_in, out_w.T)


def solution(mesh):
    in_specs = (P("dp", "seq", None), P("dp", None), P(), P(), P("dp", "seq", None))
    out_specs = (
        P("dp", "seq", None),
        P("dp", "seq", None),
        P(("dp", "seq"), None),
        P(None, ("dp", "seq")),
    )
    return jax.shard_map(local, mesh=mesh, in_specs=in_specs, out_specs=out_specs, check_vma=False)
```
